256 devices in a mesh: sess: 32 (over x, z), hist: 8 (over y, core).
Axes of the slice: x: 4, y: 4, z: 8, core: 2. Of those that a mesh axis runs over, the one named last changes fastest.
Arguments:
- events: bfloat16 [8, 32, 512, 1024], P('hist', 'sess'), may hold values from -12 to 12
- w_qkv: bfloat16 [1024, 3072], replicated, may hold values from -0.1875 to 0.1875
- patterns: int32 [8, 32, 512], P('hist', 'sess'), may hold values from 0 to 31, never falling along the last dimension, each value on 1 to 48 neighbouring positions
- owners: int32 [8, 32, 32], P('hist', 'sess'), may hold values from 0 to 31, as said below
- gaps: int32 [8, 32, 32], P('hist', 'sess'), may hold values from 1 to 127
- rates: float32 [16], replicated, may hold values from 0.001171875 to 0.09375
- prior_state: float32 [32, 16, 64, 64], P('sess'), may hold values from -4 to 4
Outputs:
- user_out: float32 [8, 32, 32, 1024], P('hist', 'sess')
The draws below stay inside these ranges and needn't reach their ends.
Inputs may be any that keep to these rules, and one draw needn't show every extreme that they name: `patterns`: every id of 0 to 31 occurs in each pack, ids never fall along a pack, each session has 1 to 48 events and one has exactly 48. `owners`: no user owns more than 2 sessions of one pack. In every history segment one user owns exactly 2 sessions of every pack of that segment.
All inputs are finite; a program needn't handle non-finite values.
Results may differ from the reference program's by a relative error of at most 0.0035.
Values sent between devices are 32-bit elements; how exact they have to be, the bound alone decides.
No kernel may reach another device: no remote copies, remote signals or barrier semaphores. Data moves between devices by JAX's collectives and lax.ppermute only.
A program may use at most 128 MiB of HBM per device.

```python
import math
import jax
import jax.numpy as jnp
import numpy as np
from jax import lax

D = 1024
HEADS = 16
HD = 64
L = 512
SPP = 32
MOSTLEN = 48
SEGS = 8
PACKS_SEG = 32
USERS = 32
CAP = 2
ROWS_DEV = 32
VISITS_EACH_ACCT = 256
GAPS = 128


def draw_events(key, part):
    key = jax.random.fold_in(key, 1)
    first = jax.random.fold_in(key, 0)
    tensor_dimensions = (SEGS, PACKS_SEG, L, D)
    values = jnp.clip(jax.random.normal(first, tensor_dimensions, jnp.float32), -6.0, 6.0)
    return values.astype(jnp.bfloat16)


def draw_owners(key, part):
    key = jax.random.fold_in(key, 2)
    hot_key, pack_key = jax.random.split(key)
    hot_users = jax.random.randint(hot_key, (SEGS,), 0, USERS)
    pack_keys = jax.random.split(pack_key, SEGS * PACKS_SEG)
    hot_each = jnp.repeat(hot_users, PACKS_SEG)

    def one_pack(pack_seed, hot_user):
        order_key, shuffle_key = jax.random.split(pack_seed)
        order = jax.random.permutation(order_key, USERS * CAP)
        slot_ids = jnp.arange(USERS * CAP, dtype=jnp.int32)
        priority = jnp.where(slot_ids // CAP == hot_user, slot_ids % CAP - CAP, order)
        picked = jnp.argsort(priority)[:SPP]
        users = (picked // CAP).astype(jnp.int32)
        return jax.random.permutation(shuffle_key, users)
    owned = jax.vmap(one_pack)(pack_keys, hot_each)
    return owned.reshape(SEGS, PACKS_SEG, SPP).astype(jnp.int32)


def draw_gaps(key, part):
    key = jax.random.fold_in(key, 3)
    floor_seed, spike_draw_seed, ceiling_draw_seed, position_seed = jax.random.split(key, 4)
    tensor_dimensions = (SEGS, PACKS_SEG, SPP)
    floor_frequency = jax.random.randint(floor_seed, tensor_dimensions, 1, 4)
    spike_frequency = jax.random.randint(spike_draw_seed, tensor_dimensions, 0, max(VISITS_EACH_ACCT // 4, 2)) == 0
    ceiling_frequency = jax.random.randint(ceiling_draw_seed, tensor_dimensions, GAPS // 2, GAPS)
    collapsed_entries = jnp.where(spike_frequency, ceiling_frequency, floor_frequency).reshape(-1)
    spot = jax.random.randint(position_seed, (), 0, collapsed_entries.shape[0])
    collapsed_entries = collapsed_entries.at[spot].set(GAPS - 1)
    return collapsed_entries.reshape(tensor_dimensions).astype(jnp.int32)


def draw_rates(key, part):
    key = jax.random.fold_in(key, 4)
    pick_key, slow_key, fast_key = jax.random.split(key, 3)
    slow_count = HEADS // 2
    ranking = jax.random.permutation(pick_key, HEADS)
    slow_heads = ranking < slow_count
    slow_part = jax.random.uniform(slow_key, (HEADS,), jnp.float32)
    fast_part = jax.random.uniform(fast_key, (HEADS,), jnp.float32)
    slow_rate = jnp.exp(jnp.log(0.3 / VISITS_EACH_ACCT) + slow_part * jnp.log(0.8 / 0.3))
    fast_rate = jnp.exp(jnp.log(0.4 / ROWS_DEV) + fast_part * jnp.log(7.5))
    return jnp.where(slow_heads, slow_rate, fast_rate).astype(jnp.float32)


def levels(stream_key, shape, cuts, low, high):
    level, own = 1.0, jax.random.fold_in(stream_key, 6)
    for dim, shards_of in cuts:
        heights = jnp.exp(jax.random.uniform(jax.random.fold_in(own, dim), (shards_of,), jnp.float32, low / len(cuts), high / len(cuts)))
        level = level * jnp.repeat(heights, shape[dim] // shards_of).reshape([-1 if axis == dim else 1 for axis in range(len(shape))])
    return level


def length_profile(number_of, total, limit, slope):
    loads = [(1 << 20) // math.isqrt(grade ** slope) + 1 for grade in range(2, number_of + 1)]
    spare, given = total - limit - (number_of - 1), [1] * (number_of - 1)
    while spare > 0:
        movable = [i for i in range(number_of - 1) if given[i] < limit]
        whole, budget = sum([loads[i] for i in movable]), spare
        for i in movable:
            addition = min(limit - given[i], max(1, budget * loads[i] // whole), spare)
            given[i] = given[i] + addition
            spare = spare - addition
    return np.array([limit] + given)


def ragged(key, amount, total, bound, slope):
    if amount == 2:
        one = jax.random.randint(key, (), max(1, total - bound), min(bound, total - 1) + 1)
        return jnp.stack([one, total - one])
    tallies = jnp.asarray(length_profile(amount, total, bound, slope), jnp.int32)
    pairs = (amount - 1) // 2
    source_of, taker = tallies[1:1 + 2 * pairs:2], tallies[2:2 + 2 * pairs:2]
    slack = jnp.minimum(source_of - 1, bound - taker)
    moved = jax.random.randint(jax.random.fold_in(key, 1), (pairs,), 0, 1 << 20) % (slack + 1)
    tallies = tallies.at[1:1 + 2 * pairs:2].set(source_of - moved).at[2:2 + 2 * pairs:2].set(taker + moved)
    return tallies[jax.random.permutation(jax.random.fold_in(key, 2), amount)]


def bell_draw(stream_key, dims, spread, bound, cuts=(), kind=jnp.bfloat16):
    drawn = jax.random.normal(stream_key, dims, jnp.float32) * spread
    if len(cuts) > 0:
        drawn = levels(stream_key, dims, cuts, -0.22, 0.18) * drawn
    return jnp.clip(drawn, min=-bound, max=bound).astype(kind)


def setup_inputs(seed: int = 0) -> dict:
    streams_of = jax.random.split(jax.random.key(seed), 8)
    return {
        "events": draw_events(jax.random.fold_in(streams_of[7], 71), 0),
        "w_qkv": bell_draw(streams_of[1], (D, 3 * D), D ** -0.5, 0.1875),
        "patterns": jax.vmap(lambda own: jnp.searchsorted(jnp.cumsum(ragged(own, SPP, L, MOSTLEN, 2)), jnp.arange(L), side="right"))(jax.random.split(streams_of[2], SEGS * PACKS_SEG)).reshape((SEGS, PACKS_SEG, L)).astype(jnp.int32),
        "owners": draw_owners(jax.random.fold_in(streams_of[7], 71), 0),
        "gaps": draw_gaps(jax.random.fold_in(streams_of[7], 71), 0),
        "rates": draw_rates(jax.random.fold_in(streams_of[7], 71), 0),
        "prior_state": bell_draw(streams_of[6], (USERS, HEADS, HD, HD), 0.5, 4.0, ((0, 32),), jnp.float32),
    }


def round_bf(values):
    return lax.optimization_barrier(values.astype(jnp.bfloat16)).astype(jnp.float32)


def encode_pack(pack_events, pack_ids, w_qkv):
    mixed = jnp.dot(pack_events, w_qkv, preferred_element_type=jnp.float32)
    query_b = round_bf(mixed[:, :D]).reshape(L, HEADS, HD)
    key_b = round_bf(mixed[:, D:2 * D]).reshape(L, HEADS, HD)
    value_b = round_bf(mixed[:, 2 * D:]).reshape(L, HEADS, HD)
    scores = jnp.einsum("qhd,khd->hqk", query_b, key_b, precision=lax.Precision.HIGHEST) * (HD ** -0.5)
    same_session = pack_ids[:, None] == pack_ids[None, :]
    scores = jnp.where(same_session[None], scores, -jnp.inf)
    peak = jnp.max(scores, axis=-1, keepdims=True)
    expd = jnp.exp(scores - peak)
    probs = expd / jnp.sum(expd, axis=-1, keepdims=True)
    probs_b = round_bf(probs)
    attended = jnp.einsum("hqk,khd->qhd", probs_b, value_b, precision=lax.Precision.HIGHEST).reshape(L, D)
    members = (pack_ids[None, :] == jnp.arange(SPP, dtype=jnp.int32)[:, None]).astype(jnp.float32)
    counts = jnp.sum(members, axis=1, keepdims=True)
    stacked = jnp.concatenate([attended, mixed[:, D:]], axis=1)
    return jnp.dot(members, stacked, precision=lax.Precision.HIGHEST) / counts


def reference(events, w_qkv, patterns, owners, gaps, rates, prior_state):
    flat_events = events.reshape(SEGS * PACKS_SEG, L, D)
    flat_ids = patterns.reshape(SEGS * PACKS_SEG, L)

    def encode_item(inputs):
        return encode_pack(inputs[0], inputs[1], w_qkv)

    summaries = lax.map(encode_item, (flat_events, flat_ids))
    rows = summaries.reshape(SEGS * PACKS_SEG * SPP, 3 * D)
    fades = jnp.exp(-rates[None, :] * gaps.reshape(-1)[:, None].astype(jnp.float32))
    user_ids = owners.reshape(-1).astype(jnp.int32)

    def advance(states, entry):
        user, summary, fade = entry
        state = lax.dynamic_index_in_dim(states, user, 0, keepdims=False)
        head_q = summary[:D].reshape(HEADS, HD)
        head_k = summary[D:2 * D].reshape(HEADS, HD)
        head_v = summary[2 * D:].reshape(HEADS, HD)
        state = fade[:, None, None] * state + head_k[:, :, None] * head_v[:, None, :]
        result = jnp.einsum("hd,hde->he", head_q, state, precision=lax.Precision.HIGHEST).reshape(D)
        states = lax.dynamic_update_index_in_dim(states, state, user, 0)
        return states, result

    final_states, outputs = lax.scan(advance, prior_state, (user_ids, rows, fades))
    return outputs.reshape(SEGS, PACKS_SEG, SPP, D)
```

```python
import functools

import jax
import jax.numpy as jnp
from jax import lax
from jax.experimental import pallas as pl
from jax.experimental.pallas import tpu as pltpu
from jax.sharding import PartitionSpec as P

HEADS = 16
SPP = 32
LONGEST = 48
HALO = 64
QUERIES = 128
PARTS = 7
BF16 = jnp.bfloat16
F32 = jnp.float32
NT = (((1,), (1,)), ((), ()))
TN = (((0,), (0,)), ((), ()))


def iota(shape, dim):
    return lax.broadcasted_iota(jnp.int32, shape, dim)


def mm(a, b, dims=(((1,), (0,)), ((), ()))):
    return lax.dot_general(a, b, dims, preferred_element_type=F32)


def split(x):
    high = x.astype(BF16)
    return high, (x - high.astype(F32)).astype(BF16)


def mm3(a, b, dims=(((1,), (0,)), ((), ()))):
    a_high, a_low = split(a)
    b_high, b_low = split(b)
    return mm(a_high, b_high, dims) + (mm(a_low, b_high, dims) + mm(a_high, b_low, dims))


def slots_of(owner_row, users):
    owned = owner_row == iota((users, SPP), 0)
    earlier = (iota((SPP, SPP), 0) < iota((SPP, SPP), 1)).astype(BF16)
    before = mm(owned.astype(F32).astype(BF16), earlier)
    return [(owned & (before == float(rank))).astype(F32) for rank in range(2)]


def windows(length):
    result = []
    for start in range(0, length, QUERIES):
        low, high = max(0, start - HALO), min(length, start + QUERIES + HALO)
        result.append((start, low, high - low))
    return result


def encode_kernel(
    users,
    groups,
    events_ref,
    wq_ref,
    wk_ref,
    wv_ref,
    pattern_ref,
    owner_ref,
    gap_ref,
    out_ref,
    mask_ref,
    place_ref,
    inverse_ref,
    weight_ref,
):
    step = pl.program_id(0)
    length = events_ref.shape[0]
    columns = wq_ref.shape[1]
    here = columns // 64

    @pl.when(step == 0)
    def _():
        pattern = pattern_ref[...]
        members = (pattern == iota((SPP, length), 0)).astype(F32).astype(BF16)
        slots = slots_of(owner_ref[...], users)
        place = mm(jnp.concatenate(slots, axis=0).astype(BF16), members)
        place_ref[...] = place.astype(BF16)
        counts = jnp.sum(place, axis=1, keepdims=True)
        inverse_ref[...] = jnp.broadcast_to(1.0 / jnp.maximum(counts, 1.0), inverse_ref.shape)
        ids = iota((SPP, QUERIES), 0).astype(F32).astype(BF16)
        id_column = mm(members, ids, TN)
        id_row = pattern.astype(F32)
        offset = 0
        for start, low, size in windows(length):
            same = id_column[low : low + size] == id_row[:, start : start + QUERIES]
            mask_ref[offset : offset + size, :] = jnp.where(same, 0.0, -jnp.inf)
            offset += size
        gap_row = gap_ref[...].astype(F32)
        gap_columns = [jnp.sum(slot * gap_row, axis=1, keepdims=True) for slot in slots]
        both = jnp.where(iota((users, 128), 1) < 64, gap_columns[0], gap_columns[1])
        for group in range(groups):
            out_ref[pl.ds(group * users * PARTS + 6, users, stride=PARTS), :] = both

    events = events_ref[...]
    query = mm(events, wq_ref[...]).astype(BF16)
    key = mm(events, wk_ref[...])
    value = mm(events, wv_ref[...])
    key_b = key.astype(BF16)
    head_of = iota((1, columns), 1) // 64
    only = [jnp.where(head_of == head, 0.125, 0.0).astype(BF16) for head in range(here)]
    spread = (
        (iota((here * QUERIES, columns), 0) // QUERIES == iota((here * QUERIES, columns), 1) // 64)
        .astype(F32)
        .astype(BF16)
    )
    weight_ref[...] = jnp.zeros_like(weight_ref)
    offset = 0
    for start, low, size in windows(length):
        block = query[start : start + QUERIES]
        stacked = jnp.concatenate([block * keep for keep in only], axis=0)
        scores = mm(key_b[low : low + size], stacked, NT)
        mask = mask_ref[offset : offset + size, :]
        offset += size
        probs = []
        for head in range(here):
            part = scores[:, head * QUERIES : (head + 1) * QUERIES] + mask
            expd = jnp.exp(part - jnp.max(part, axis=0, keepdims=True))
            probs.append((expd * (1.0 / jnp.sum(expd, axis=0, keepdims=True))).astype(BF16))
        weight_ref[low : low + size, :] += mm(jnp.concatenate(probs, axis=1), spread)
    weighted = weight_ref[...] * value.astype(BF16).astype(F32)
    place = place_ref[...]
    inverse = inverse_ref[...]
    for part, rows in enumerate((weighted, key, value)):
        high, low = split(rows)
        means = mm(place, high) + mm(place, low)
        for sub in range(columns // 128):
            group = step * (columns // 128) + sub
            for rank in range(2):
                out_ref[pl.ds(group * users * PARTS + part * 2 + rank, users, stride=PARTS), :] = (
                    means[rank * users : (rank + 1) * users, sub * 128 : (sub + 1) * 128]
                    * inverse[rank * users : (rank + 1) * users]
                )


def encode(events, w_qkv, patterns, owners, gaps, users, groups):
    length, width = events.shape
    columns = 256
    steps = width // columns
    window_rows = sum(size for _, _, size in windows(length))
    rows = groups * users * PARTS
    whole = lambda shape: pl.BlockSpec(shape, lambda i: (0, 0))
    column = lambda part: pl.BlockSpec((width, columns), lambda i: (0, part * steps + i))
    return pl.pallas_call(
        functools.partial(encode_kernel, users, groups),
        grid=(steps,),
        in_specs=[
            whole((length, width)),
            column(0),
            column(1),
            column(2),
            whole((1, length)),
            whole((1, SPP)),
            whole((1, SPP)),
        ],
        out_specs=whole((rows, 128)),
        out_shape=jax.ShapeDtypeStruct((rows, 128), F32),
        scratch_shapes=[
            pltpu.VMEM((window_rows, QUERIES), F32),
            pltpu.VMEM((2 * users, length), BF16),
            pltpu.VMEM((2 * users, 128), F32),
            pltpu.VMEM((length, columns), F32),
        ],
        compiler_params=pltpu.CompilerParams(vmem_limit_bytes=40 * 1024 * 1024),
        name="encode",
    )(events, w_qkv, w_qkv, w_qkv, patterns, owners, gaps)


def recur_kernel(packs, group_ref, rates_ref, rows_ref, prior_ref, out_ref):
    group = group_ref[0]
    rate = [rates_ref[2 * group], rates_ref[2 * group + 1]]
    rows = 2 * packs
    load = lambda part: rows_ref[pl.ds(part, packs, stride=PARTS), :]
    both = lambda part: jnp.concatenate([load(part), load(part + 1)], axis=0)
    query, key, value = both(0), both(2), both(4)
    first = iota((rows, 128), 1) < 64
    gap = load(6)
    turned = pltpu.roll(gap, 64, 1)
    gap = jnp.concatenate(
        [jnp.where(first[:packs], gap, turned), jnp.where(first[:packs], turned, gap)], axis=0
    ).astype(BF16)
    time = lambda dim: (
        lambda n: jnp.where(n >= packs, 2 * (n - packs) + 1, 2 * n)
    )(iota((rows, rows), dim))
    causal = time(0) >= time(1)
    elapsed = mm(causal.astype(F32).astype(BF16), gap)
    elapsed_row = elapsed.T[0:1, :]
    since = jnp.where(causal, elapsed[:, 0:1] - elapsed_row, 1e30)
    key_high, key_low = split(key)
    value_high, value_low = split(value)
    result = None
    for head in range(2):
        mine = first if head == 0 else jnp.logical_not(first)
        q_high, q_low = split(jnp.where(mine, query, 0.0))
        scores = mm(q_high, key_high, NT) + (mm(q_low, key_high, NT) + mm(q_high, key_low, NT))
        scores = scores * jnp.exp(-rate[head] * since)
        s_high, s_low = split(scores)
        local = mm(s_high, value_high) + (mm(s_low, value_high) + mm(s_high, value_low))
        result = local if head == 0 else jnp.where(first, result, local)
    lane_rate = jnp.where(first, rate[0], rate[1])
    faded = query * jnp.exp(-lane_rate * elapsed)
    empty = jnp.zeros((64, 64), F32)
    prior = jnp.concatenate(
        [
            jnp.concatenate([prior_ref[0], empty], axis=1),
            jnp.concatenate([empty, prior_ref[1]], axis=1),
        ],
        axis=0,
    )
    result = result + mm3(faded, prior)
    for rank in range(2):
        out_ref[pl.ds(rank, packs, stride=2), :] = result[rank * packs : (rank + 1) * packs]


def recur(group, rates, rows, prior, packs):
    return pl.pallas_call(
        functools.partial(recur_kernel, packs),
        grid_spec=pltpu.PrefetchScalarGridSpec(
            num_scalar_prefetch=2,
            grid=(1,),
            in_specs=[
                pl.BlockSpec(rows.shape, lambda i, group, rates: (0, 0)),
                pl.BlockSpec((2, 64, 64), lambda i, group, rates: (group[0], 0, 0)),
            ],
            out_specs=pl.BlockSpec((2 * packs, 128), lambda i, group, rates: (0, 0)),
        ),
        out_shape=jax.ShapeDtypeStruct((2 * packs, 128), F32),
        compiler_params=pltpu.CompilerParams(vmem_limit_bytes=40 * 1024 * 1024),
        name="recur",
    )(group, rates, rows, prior)


def pick_kernel(users, groups, owner_ref, rows_ref, out_ref):
    slots = jnp.concatenate(slots_of(owner_ref[...], users), axis=0).astype(BF16)
    for group in range(groups):
        mine = jnp.concatenate(
            [rows_ref[pl.ds(group * users * 2 + rank, users, stride=2), :] for rank in range(2)],
            axis=0,
        )
        high = mine.astype(BF16)
        rest = mine - high.astype(F32)
        middle, low = split(rest)
        out_ref[:, group * 128 : (group + 1) * 128] = mm(slots, high, TN) + (
            mm(slots, middle, TN) + mm(slots, low, TN)
        )


def pick(owners, rows, users, groups):
    return pl.pallas_call(
        functools.partial(pick_kernel, users, groups),
        out_shape=jax.ShapeDtypeStruct((SPP, groups * 128), F32),
        compiler_params=pltpu.CompilerParams(vmem_limit_bytes=16 * 1024 * 1024),
        name="pick",
    )(owners, rows)


def shards(events, w_qkv, patterns, owners, gaps, rates, prior_state):
    groups = lax.axis_size("hist")
    users = lax.axis_size("sess")
    packs = groups * users
    axes = ("hist", "sess")
    send = encode(events[0, 0], w_qkv, patterns[0], owners[0], gaps[0], users, groups)
    arrived = lax.all_to_all(
        send.reshape(packs, PARTS, 1, 128), axes, split_axis=0, concat_axis=0, tiled=True
    ).reshape(packs * PARTS, 128)
    group = lax.axis_index("hist").astype(jnp.int32).reshape(1)
    done = recur(group, rates, arrived, prior_state[0], packs)
    returned = lax.all_to_all(
        done.reshape(packs, 2, 128), axes, split_axis=0, concat_axis=0, tiled=True
    ).reshape(packs * 2, 128)
    return pick(owners[0], returned, users, groups)[None, None]


def solution(mesh):
    placed = (
        P("hist", "sess", None, None),
        P(),
        P("hist", "sess", None),
        P("hist", "sess", None),
        P("hist", "sess", None),
        P(),
        P("sess", None, None, None),
    )
    return jax.shard_map(
        shards, mesh=mesh, in_specs=placed, out_specs=P("hist", "sess", None, None), check_vma=False
    )
```

```python
import functools

import jax
import jax.numpy as jnp
from jax import lax
from jax.experimental import pallas as pl
from jax.experimental.pallas import tpu as pltpu
from jax.sharding import PartitionSpec as P

HEADS = 16
SPP = 32
LONGEST = 48
QUERIES = 64
PARTS = 7
BF16 = jnp.bfloat16
F32 = jnp.float32
NT = (((1,), (1,)), ((), ()))
TN = (((0,), (0,)), ((), ()))


def iota(shape, dim):
    return lax.broadcasted_iota(jnp.int32, shape, dim)


def mm(a, b, dims=(((1,), (0,)), ((), ()))):
    return lax.dot_general(a, b, dims, preferred_element_type=F32)


def split(x):
    high = x.astype(BF16)
    return high, (x - high.astype(F32)).astype(BF16)


def mm3(a, b, dims=(((1,), (0,)), ((), ()))):
    a_high, a_low = split(a)
    b_high, b_low = split(b)
    return mm(a_high, b_high, dims) + (mm(a_low, b_high, dims) + mm(a_high, b_low, dims))


def slots_of(owner_row, users):
    owned = owner_row == iota((users, SPP), 0)
    earlier = (iota((SPP, SPP), 0) < iota((SPP, SPP), 1)).astype(BF16)
    before = mm(owned.astype(F32).astype(BF16), earlier)
    return [(owned & (before == float(rank))).astype(F32) for rank in range(2)]


def windows(length):
    result = []
    for start in range(0, length, QUERIES):
        low, high = max(0, start - LONGEST), min(length, start + QUERIES + LONGEST)
        result.append((start, low, high - low))
    return result


def encode_kernel(
    users,
    groups,
    events_hbm,
    w_hbm,
    pattern_hbm,
    owner_hbm,
    gap_hbm,
    out_ref,
    rows_ref,
    w_ref,
    pattern_ref,
    owner_ref,
    gap_ref,
    mask_ref,
    query_ref,
    key_ref,
    value_ref,
    weight_ref,
    small_sem,
    events_sem,
    w_sem,
):
    length, width = events_hbm.shape
    columns = 256
    here = columns // 64
    steps = width // columns
    small = [
        pltpu.make_async_copy(source, target, small_sem.at[n])
        for n, (source, target) in enumerate(
            [(pattern_hbm, pattern_ref), (owner_hbm, owner_ref), (gap_hbm, gap_ref)]
        )
    ]
    in_events = pltpu.make_async_copy(events_hbm, rows_ref.at[0:length], events_sem)
    in_w = [
        [
            pltpu.make_async_copy(
                w_hbm.at[:, part * width + step * columns : part * width + (step + 1) * columns],
                w_ref.at[step * 3 + part],
                w_sem.at[step * 3 + part],
            )
            for part in range(3)
        ]
        for step in range(steps)
    ]
    for copy in small:
        copy.start()
    in_events.start()
    for copies in in_w:
        for copy in copies:
            copy.start()
    for copy in small:
        copy.wait()

    pattern = pattern_ref[...]
    members = (pattern == iota((SPP, length), 0)).astype(F32).astype(BF16)
    slots = slots_of(owner_ref[...], users)
    place = mm(jnp.concatenate(slots, axis=0).astype(BF16), members)
    counts = jnp.sum(place, axis=1, keepdims=True)
    place = place.astype(BF16)
    inverse = jnp.broadcast_to(1.0 / jnp.maximum(counts, 1.0), (2 * users, columns))
    ids = iota((SPP, 128), 0).astype(F32).astype(BF16)
    id_column = mm(members, ids, TN)
    id_row = pattern.astype(F32)
    offset = 0
    for start, low, size in windows(length):
        block = id_row[:, start : start + QUERIES]
        same = id_column[low : low + size] == jnp.concatenate([block, block], axis=1)
        mask_ref[offset : offset + size, :] = jnp.where(same, 0.0, -jnp.inf)
        offset += size
    gap_row = gap_ref[...].astype(F32)
    gap_columns = [jnp.sum(slot * gap_row, axis=1, keepdims=True) for slot in slots]
    both = jnp.where(iota((users, 128), 1) < 64, gap_columns[0], gap_columns[1])
    for group in range(groups):
        out_ref[pl.ds(group * users * PARTS + 6, users, stride=PARTS), :] = both

    head_of = iota((1, columns), 1) // 64
    only = [jnp.where(head_of == head, 0.125, 0.0).astype(BF16) for head in range(here)]
    spread = (
        (iota((columns, columns), 0) // QUERIES == iota((columns, columns), 1) // 64)
        .astype(F32)
        .astype(BF16)
    )

    in_events.wait()
    high, low = split(mm(place, rows_ref[0:length, :]))
    rows_ref[length : length + 2 * users, :] = high
    rows_ref[length + 2 * users :, :] = low

    def store(step, part, means):
        for sub in range(columns // 128):
            group = step * (columns // 128) + sub
            for rank in range(2):
                out_ref[
                    pl.ds(group * users * PARTS + part * 2 + rank, users, stride=PARTS), :
                ] = means[rank * users : (rank + 1) * users, sub * 128 : (sub + 1) * 128]

    def project(step):
        query_ref[step] = mm(rows_ref[0:length, :], w_ref[step * 3]).astype(BF16)
        for part, target in ((1, key_ref), (2, value_ref)):
            mixed = mm(rows_ref[...], w_ref[step * 3 + part])
            means = mixed[length : length + 2 * users] + mixed[length + 2 * users :]
            store(step, part, means * inverse)
            target[step] = mixed[:length].astype(BF16)

    def attend(step):
        offset = 0
        reached = 0
        for start, low, size in windows(length):
            block = query_ref[step, start : start + QUERIES, :]
            stacked = jnp.concatenate([block * keep for keep in only], axis=0)
            scores = mm(key_ref[step, low : low + size, :], stacked, NT)
            mask = mask_ref[offset : offset + size, :]
            offset += size
            probs = []
            for half in range(columns // 128):
                part = scores[:, half * 128 : (half + 1) * 128] + mask
                expd = jnp.exp(part - jnp.max(part, axis=0, keepdims=True))
                probs.append(expd * (1.0 / jnp.sum(expd, axis=0, keepdims=True)))
            probs = jnp.concatenate(probs, axis=1)
            known = reached - low
            if known:
                weight_ref[step, low:reached, :] += probs[:known]
            weight_ref[step, reached : low + size, :] = probs[known:]
            reached = low + size

    def finish(step):
        weight = mm(weight_ref[step].astype(BF16), spread)
        high, low = split(weight * value_ref[step].astype(F32))
        store(step, 0, (mm(place, high) + mm(place, low)) * inverse)

    for copies in in_w:
        for copy in copies:
            copy.wait()
    for step in range(steps):
        project(step)
    for step in range(steps):
        attend(step)
    for step in range(steps):
        finish(step)


def encode(events, w_qkv, patterns, owners, gaps, users, groups):
    length, width = events.shape
    columns = 256
    steps = width // columns
    window_rows = sum(size for _, _, size in windows(length))
    rows = groups * users * PARTS
    return pl.pallas_call(
        functools.partial(encode_kernel, users, groups),
        in_specs=[pl.BlockSpec(memory_space=pl.ANY)] * 5,
        out_shape=jax.ShapeDtypeStruct((rows, 128), F32),
        scratch_shapes=[
            pltpu.VMEM((length + 4 * users, width), BF16),
            pltpu.VMEM((3 * steps, width, columns), BF16),
            pltpu.VMEM((1, length), jnp.int32),
            pltpu.VMEM((1, SPP), jnp.int32),
            pltpu.VMEM((1, SPP), jnp.int32),
            pltpu.VMEM((window_rows, 128), F32),
            pltpu.VMEM((steps, length, columns), BF16),
            pltpu.VMEM((steps, length, columns), BF16),
            pltpu.VMEM((steps, length, columns), BF16),
            pltpu.VMEM((steps, length, columns), F32),
            pltpu.SemaphoreType.DMA((3,)),
            pltpu.SemaphoreType.DMA,
            pltpu.SemaphoreType.DMA((3 * steps,)),
        ],
        compiler_params=pltpu.CompilerParams(vmem_limit_bytes=60 * 1024 * 1024),
        name="encode",
    )(events, w_qkv, patterns, owners, gaps)


def recur_kernel(packs, group_ref, rates_ref, rows_ref, prior_ref, out_ref):
    group = group_ref[0]
    rate = [rates_ref[2 * group], rates_ref[2 * group + 1]]
    rows = 2 * packs
    load = lambda part: rows_ref[pl.ds(part, packs, stride=PARTS), :]
    both = lambda part: jnp.concatenate([load(part), load(part + 1)], axis=0)
    query, key, value = both(0), both(2), both(4)
    first = iota((rows, 128), 1) < 64
    gap = load(6)
    turned = pltpu.roll(gap, 64, 1)
    gap = jnp.concatenate(
        [jnp.where(first[:packs], gap, turned), jnp.where(first[:packs], turned, gap)], axis=0
    ).astype(BF16)
    time = lambda dim: (
        lambda n: jnp.where(n >= packs, 2 * (n - packs) + 1, 2 * n)
    )(iota((rows, rows), dim))
    causal = time(0) >= time(1)
    elapsed = mm(causal.astype(F32).astype(BF16), gap)
    elapsed_row = elapsed.T[0:1, :]
    since = jnp.where(causal, elapsed[:, 0:1] - elapsed_row, 1e30)
    key_high, key_low = split(key)
    value_high, value_low = split(value)
    result = None
    for head in range(2):
        mine = first if head == 0 else jnp.logical_not(first)
        q_high, q_low = split(jnp.where(mine, query, 0.0))
        scores = mm(q_high, key_high, NT) + (mm(q_low, key_high, NT) + mm(q_high, key_low, NT))
        scores = scores * jnp.exp(-rate[head] * since)
        s_high, s_low = split(scores)
        local = mm(s_high, value_high) + (mm(s_low, value_high) + mm(s_high, value_low))
        result = local if head == 0 else jnp.where(first, result, local)
    lane_rate = jnp.where(first, rate[0], rate[1])
    faded = query * jnp.exp(-lane_rate * elapsed)
    empty = jnp.zeros((64, 64), F32)
    prior = jnp.concatenate(
        [
            jnp.concatenate([prior_ref[0], empty], axis=1),
            jnp.concatenate([empty, prior_ref[1]], axis=1),
        ],
        axis=0,
    )
    result = result + mm3(faded, prior)
    for rank in range(2):
        out_ref[pl.ds(rank, packs, stride=2), :] = result[rank * packs : (rank + 1) * packs]


def recur(group, rates, rows, prior, packs):
    return pl.pallas_call(
        functools.partial(recur_kernel, packs),
        grid_spec=pltpu.PrefetchScalarGridSpec(
            num_scalar_prefetch=2,
            grid=(1,),
            in_specs=[
                pl.BlockSpec(rows.shape, lambda i, group, rates: (0, 0)),
                pl.BlockSpec((2, 64, 64), lambda i, group, rates: (group[0], 0, 0)),
            ],
            out_specs=pl.BlockSpec((2 * packs, 128), lambda i, group, rates: (0, 0)),
        ),
        out_shape=jax.ShapeDtypeStruct((2 * packs, 128), F32),
        compiler_params=pltpu.CompilerParams(vmem_limit_bytes=40 * 1024 * 1024),
        name="recur",
    )(group, rates, rows, prior)


def pick_kernel(users, groups, owner_ref, rows_ref, out_ref):
    slots = jnp.concatenate(slots_of(owner_ref[...], users), axis=0).astype(BF16)
    for group in range(groups):
        mine = jnp.concatenate(
            [rows_ref[pl.ds(group * users * 2 + rank, users, stride=2), :] for rank in range(2)],
            axis=0,
        )
        high = mine.astype(BF16)
        rest = mine - high.astype(F32)
        middle, low = split(rest)
        out_ref[:, group * 128 : (group + 1) * 128] = mm(slots, high, TN) + (
            mm(slots, middle, TN) + mm(slots, low, TN)
        )


def pick(owners, rows, users, groups):
    return pl.pallas_call(
        functools.partial(pick_kernel, users, groups),
        out_shape=jax.ShapeDtypeStruct((SPP, groups * 128), F32),
        compiler_params=pltpu.CompilerParams(vmem_limit_bytes=16 * 1024 * 1024),
        name="pick",
    )(owners, rows)


def shards(events, w_qkv, patterns, owners, gaps, rates, prior_state):
    groups = lax.axis_size("hist")
    users = lax.axis_size("sess")
    packs = groups * users
    axes = ("hist", "sess")
    send = encode(events[0, 0], w_qkv, patterns[0], owners[0], gaps[0], users, groups)
    arrived = lax.all_to_all(
        send.reshape(packs, PARTS, 1, 128), axes, split_axis=0, concat_axis=0, tiled=True
    ).reshape(packs * PARTS, 128)
    group = lax.axis_index("hist").astype(jnp.int32).reshape(1)
    done = recur(group, rates, arrived, prior_state[0], packs)
    returned = lax.all_to_all(
        done.reshape(packs, 2, 128), axes, split_axis=0, concat_axis=0, tiled=True
    ).reshape(packs * 2, 128)
    return pick(owners[0], returned, users, groups)[None, None]


def solution(mesh):
    placed = (
        P("hist", "sess", None, None),
        P(),
        P("hist", "sess", None),
        P("hist", "sess", None),
        P("hist", "sess", None),
        P(),
        P("sess", None, None, None),
    )
    return jax.shard_map(
        shards, mesh=mesh, in_specs=placed, out_specs=P("hist", "sess", None, None), check_vma=False
    )
```

```python
import functools

import jax
import jax.numpy as jnp
from jax import lax
from jax.experimental import pallas as pl
from jax.experimental.pallas import tpu as pltpu
from jax.sharding import PartitionSpec as P

HEADS = 16
SPP = 32
LONGEST = 48
QUERIES = 64
PARTS = 7
BF16 = jnp.bfloat16
F32 = jnp.float32
NT = (((1,), (1,)), ((), ()))
TN = (((0,), (0,)), ((), ()))


def iota(shape, dim):
    return lax.broadcasted_iota(jnp.int32, shape, dim)


def mm(a, b, dims=(((1,), (0,)), ((), ()))):
    return lax.dot_general(a, b, dims, preferred_element_type=F32)


def split(x):
    high = x.astype(BF16)
    return high, (x - high.astype(F32)).astype(BF16)


def mm3(a, b, dims=(((1,), (0,)), ((), ()))):
    a_high, a_low = split(a)
    b_high, b_low = split(b)
    return mm(a_high, b_high, dims) + (mm(a_low, b_high, dims) + mm(a_high, b_low, dims))


def slots_of(owner_row, users):
    owned = owner_row == iota((users, SPP), 0)
    earlier = (iota((SPP, SPP), 0) < iota((SPP, SPP), 1)).astype(BF16)
    before = mm(owned.astype(F32).astype(BF16), earlier)
    return [(owned & (before == float(rank))).astype(F32) for rank in range(2)]


def windows(length):
    result = []
    for start in range(0, length, QUERIES):
        low, high = max(0, start - LONGEST), min(length, start + QUERIES + LONGEST)
        result.append((start, low, high - low))
    return result


def encode_kernel(
    users,
    groups,
    events_hbm,
    w_hbm,
    pattern_hbm,
    owner_hbm,
    gap_hbm,
    out_ref,
    rows_ref,
    w_ref,
    pattern_ref,
    owner_ref,
    gap_ref,
    mask_ref,
    query_ref,
    key_ref,
    value_ref,
    weight_ref,
    small_sem,
    events_sem,
    w_sem,
):
    length, width = events_hbm.shape
    columns = 256
    here = columns // 64
    steps = width // columns
    small = [
        pltpu.make_async_copy(source, target, small_sem.at[n])
        for n, (source, target) in enumerate(
            [(pattern_hbm, pattern_ref), (owner_hbm, owner_ref), (gap_hbm, gap_ref)]
        )
    ]
    in_events = pltpu.make_async_copy(events_hbm, rows_ref.at[0:length], events_sem)
    in_w = [
        [
            pltpu.make_async_copy(
                w_hbm.at[:, part * width + step * columns : part * width + (step + 1) * columns],
                w_ref.at[step * 3 + part],
                w_sem.at[step * 3 + part],
            )
            for part in range(3)
        ]
        for step in range(steps)
    ]
    for copy in small:
        copy.start()
    in_events.start()
    for copy in in_w[0]:
        copy.start()
    for copy in small:
        copy.wait()

    pattern = pattern_ref[...]
    members = (pattern == iota((SPP, length), 0)).astype(F32).astype(BF16)
    slots = slots_of(owner_ref[...], users)
    place = mm(jnp.concatenate(slots, axis=0).astype(BF16), members)
    counts = jnp.sum(place, axis=1, keepdims=True)
    place = place.astype(BF16)
    inverse = jnp.broadcast_to(1.0 / jnp.maximum(counts, 1.0), (2 * users, columns))
    ids = iota((SPP, 128), 0).astype(F32).astype(BF16)
    id_column = mm(members, ids, TN)
    id_row = pattern.astype(F32)
    offset = 0
    for start, low, size in windows(length):
        block = id_row[:, start : start + QUERIES]
        same = id_column[low : low + size] == jnp.concatenate([block, block], axis=1)
        mask_ref[offset : offset + size, :] = jnp.where(same, 0.0, -jnp.inf)
        offset += size
    gap_row = gap_ref[...].astype(F32)
    gap_columns = [jnp.sum(slot * gap_row, axis=1, keepdims=True) for slot in slots]
    both = jnp.where(iota((users, 128), 1) < 64, gap_columns[0], gap_columns[1])
    for group in range(groups):
        out_ref[pl.ds(group * users * PARTS + 6, users, stride=PARTS), :] = both

    head_of = iota((1, columns), 1) // 64
    only = [jnp.where(head_of == head, 0.125, 0.0).astype(BF16) for head in range(here)]
    spread = (
        (iota((columns, columns), 0) // QUERIES == iota((columns, columns), 1) // 64)
        .astype(F32)
        .astype(BF16)
    )

    in_events.wait()
    for copies in in_w[1:]:
        for copy in copies:
            copy.start()
    high, low = split(mm(place, rows_ref[0:length, :]))
    rows_ref[length : length + 2 * users, :] = high
    rows_ref[length + 2 * users :, :] = low

    def store(step, part, means):
        for sub in range(columns // 128):
            group = step * (columns // 128) + sub
            for rank in range(2):
                out_ref[
                    pl.ds(group * users * PARTS + part * 2 + rank, users, stride=PARTS), :
                ] = means[rank * users : (rank + 1) * users, sub * 128 : (sub + 1) * 128]

    def project(step):
        for at in range(0, length, 256):
            chunk = rows_ref[at : at + 256, :]
            query_ref[step, at : at + 256, :] = mm(chunk, w_ref[step * 3]).astype(BF16)
        for part, target in ((1, key_ref), (2, value_ref)):
            for at in range(0, length, 256):
                chunk = rows_ref[at : at + 256, :]
                target[step, at : at + 256, :] = mm(chunk, w_ref[step * 3 + part]).astype(BF16)
            extra = mm(rows_ref[length:, :], w_ref[step * 3 + part])
            store(step, part, (extra[: 2 * users] + extra[2 * users :]) * inverse)

    def attend(step):
        offset = 0
        reached = 0
        for start, low, size in windows(length):
            block = query_ref[step, start : start + QUERIES, :]
            stacked = jnp.concatenate([block * keep for keep in only], axis=0)
            scores = mm(key_ref[step, low : low + size, :], stacked, NT)
            mask = mask_ref[offset : offset + size, :]
            offset += size
            probs = []
            for half in range(columns // 128):
                part = scores[:, half * 128 : (half + 1) * 128] + mask
                expd = jnp.exp(part - jnp.max(part, axis=0, keepdims=True))
                probs.append(expd * (1.0 / jnp.sum(expd, axis=0, keepdims=True)))
            probs = jnp.concatenate(probs, axis=1)
            known = reached - low
            if known:
                weight_ref[step, low:reached, :] += probs[:known]
            weight_ref[step, reached : low + size, :] = probs[known:]
            reached = low + size

    def finish(step):
        weight = mm(weight_ref[step].astype(BF16), spread)
        high, low = split(weight * value_ref[step].astype(F32))
        store(step, 0, (mm(place, high) + mm(place, low)) * inverse)

    for copy in in_w[0]:
        copy.wait()
    project(0)
    for copies in in_w[1:]:
        for copy in copies:
            copy.wait()
    project(1)
    project(2)
    project(3)
    attend(0)
    attend(1)
    attend(2)
    finish(0)
    finish(1)
    attend(3)
    finish(2)
    finish(3)


def encode(events, w_qkv, patterns, owners, gaps, users, groups):
    length, width = events.shape
    columns = 256
    steps = width // columns
    window_rows = sum(size for _, _, size in windows(length))
    rows = groups * users * PARTS
    return pl.pallas_call(
        functools.partial(encode_kernel, users, groups),
        in_specs=[pl.BlockSpec(memory_space=pl.ANY)] * 5,
        out_shape=jax.ShapeDtypeStruct((rows, 128), F32),
        scratch_shapes=[
            pltpu.VMEM((length + 4 * users, width), BF16),
            pltpu.VMEM((3 * steps, width, columns), BF16),
            pltpu.VMEM((1, length), jnp.int32),
            pltpu.VMEM((1, SPP), jnp.int32),
            pltpu.VMEM((1, SPP), jnp.int32),
            pltpu.VMEM((window_rows, 128), F32),
            pltpu.VMEM((steps, length, columns), BF16),
            pltpu.VMEM((steps, length, columns), BF16),
            pltpu.VMEM((steps, length, columns), BF16),
            pltpu.VMEM((steps, length, columns), F32),
            pltpu.SemaphoreType.DMA((3,)),
            pltpu.SemaphoreType.DMA,
            pltpu.SemaphoreType.DMA((3 * steps,)),
        ],
        compiler_params=pltpu.CompilerParams(vmem_limit_bytes=60 * 1024 * 1024),
        name="encode",
    )(events, w_qkv, patterns, owners, gaps)


def recur_kernel(packs, rates_hbm, rows_ref, prior_hbm, out_ref, rates_ref, prior_ref, sem):
    group = lax.axis_index("hist")
    in_rates = pltpu.make_async_copy(rates_hbm, rates_ref, sem.at[0])
    in_prior = pltpu.make_async_copy(prior_hbm.at[pl.ds(2 * group, 2)], prior_ref, sem.at[1])
    in_rates.start()
    in_prior.start()
    half = packs // 2
    rows = 2 * packs
    load = lambda part, late: rows_ref[pl.ds(late * half * PARTS + part, half, stride=PARTS), :]
    both = lambda part: jnp.concatenate(
        [load(part + rank, late) for late in range(2) for rank in range(2)], axis=0
    )
    first = iota((1, 128), 1) < 64

    def time(dim):
        n = iota((rows, rows), dim)
        return 2 * (n // packs * half + n % half) + n % packs // half

    gap = []
    for late in range(2):
        stored = load(6, late)
        turned = pltpu.roll(stored, 64, 1)
        gap += [jnp.where(first, stored, turned), jnp.where(first, turned, stored)]
    causal = time(0) >= time(1)
    elapsed = mm(causal.astype(F32).astype(BF16), jnp.concatenate(gap, axis=0).astype(BF16))
    since = jnp.where(causal, elapsed[:, 0:1] - elapsed.T[0:1, :], 1e30)

    query, key, value = both(0), both(2), both(4)
    turned_query, turned_key = pltpu.roll(query, 64, 1), pltpu.roll(key, 64, 1)
    value_high, value_low = split(value)
    value_both = jnp.concatenate([value_high, value_low], axis=1)
    in_rates.wait()
    in_prior.wait()
    rate = [rates_ref[2 * group], rates_ref[2 * group + 1]]

    def pieces(x):
        high = x.astype(BF16).astype(F32)
        return high, x - high

    sides = []
    for head in range(2):
        mine = first if head == 0 else jnp.logical_not(first)
        q_high, q_low = pieces(jnp.where(mine, query, turned_query))
        k_high, k_low = pieces(jnp.where(mine, key, turned_key))
        left = jnp.concatenate([jnp.where(first, q_high, q_low), jnp.where(first, q_high, 0.0)], axis=1)
        right = jnp.concatenate([k_high, jnp.where(first, k_low, 0.0)], axis=1)
        sides.append((left.astype(BF16), right.astype(BF16)))

    empty = jnp.zeros((64, 64), F32)
    prior = jnp.concatenate(
        [
            jnp.concatenate([prior_ref[0], empty], axis=1),
            jnp.concatenate([empty, prior_ref[1]], axis=1),
        ],
        axis=0,
    )
    prior_high, prior_low = split(prior)
    prior_twice = jnp.concatenate([prior_high, prior_high], axis=0)
    lane_rate = jnp.where(first, rate[0], rate[1])

    for late in range(2):
        mine = slice(late * packs, (late + 1) * packs)
        seen = slice(0, (late + 1) * packs)
        heads = []
        for head in range(2):
            left, right = sides[head]
            scores = mm(left[mine], right[seen], NT) * jnp.exp(-rate[head] * since[mine, seen])
            s_high, s_low = split(scores)
            wide = mm(s_high, value_both[seen])
            heads.append(wide[:, :128] + (wide[:, 128:] + mm(s_low, value_high[seen])))
        f_high, f_low = split(query[mine] * jnp.exp(-lane_rate * elapsed[mine]))
        carried = mm(jnp.concatenate([f_high, f_low], axis=1), prior_twice) + mm(f_high, prior_low)
        result = jnp.where(first, heads[0], heads[1]) + carried
        for rank in range(2):
            out_ref[pl.ds(late * packs + rank, half, stride=2), :] = (
                result[rank * half : (rank + 1) * half]
            )


def recur(rates, rows, prior, packs):
    return pl.pallas_call(
        functools.partial(recur_kernel, packs),
        in_specs=[
            pl.BlockSpec(memory_space=pl.ANY),
            pl.BlockSpec(memory_space=pltpu.VMEM),
            pl.BlockSpec(memory_space=pl.ANY),
        ],
        out_shape=jax.ShapeDtypeStruct((2 * packs, 128), F32),
        scratch_shapes=[
            pltpu.SMEM(rates.shape, F32),
            pltpu.VMEM((2, 64, 64), F32),
            pltpu.SemaphoreType.DMA((2,)),
        ],
        compiler_params=pltpu.CompilerParams(vmem_limit_bytes=40 * 1024 * 1024),
        name="recur",
    )(rates, rows, prior)


def pick_kernel(users, groups, owner_hbm, rows_ref, out_ref, owner_ref, sem):
    in_owner = pltpu.make_async_copy(owner_hbm, owner_ref, sem)
    in_owner.start()
    in_owner.wait()
    slots = jnp.concatenate(slots_of(owner_ref[...], users), axis=0).astype(BF16)
    mine = jnp.concatenate(
        [
            jnp.concatenate(
                [rows_ref[pl.ds(group * users * 2 + rank, users, stride=2), :] for rank in range(2)],
                axis=0,
            )
            for group in range(groups)
        ],
        axis=1,
    )
    high = mine.astype(BF16)
    middle, low = split(mine - high.astype(F32))
    out_ref[...] = mm(slots, high, TN) + (mm(slots, middle, TN) + mm(slots, low, TN))


def pick(owners, rows, users, groups):
    return pl.pallas_call(
        functools.partial(pick_kernel, users, groups),
        in_specs=[
            pl.BlockSpec(memory_space=pl.ANY),
            pl.BlockSpec(memory_space=pltpu.VMEM),
        ],
        out_shape=jax.ShapeDtypeStruct((SPP, groups * 128), F32),
        scratch_shapes=[pltpu.VMEM((1, SPP), jnp.int32), pltpu.SemaphoreType.DMA],
        compiler_params=pltpu.CompilerParams(vmem_limit_bytes=16 * 1024 * 1024),
        name="pick",
    )(owners, rows)


def shards(events, w_qkv, patterns, owners, gaps, rates, prior_state):
    groups = lax.axis_size("hist")
    users = lax.axis_size("sess")
    packs = groups * users
    axes = ("hist", "sess")
    send = encode(events[0, 0], w_qkv, patterns[0], owners[0], gaps[0], users, groups)
    arrived = lax.all_to_all(
        send.reshape(packs, PARTS, 1, 128), axes, split_axis=0, concat_axis=0, tiled=True
    ).reshape(packs * PARTS, 128)
    done = recur(rates, arrived, prior_state[0], packs)
    returned = lax.all_to_all(
        done.reshape(packs, 2, 128), axes, split_axis=0, concat_axis=0, tiled=True
    ).reshape(packs * 2, 128)
    return pick(owners[0], returned, users, groups)[None, None]


def solution(mesh):
    placed = (
        P("hist", "sess", None, None),
        P(),
        P("hist", "sess", None),
        P("hist", "sess", None),
        P("hist", "sess", None),
        P(),
        P("sess", None, None, None),
    )
    return jax.shard_map(
        shards, mesh=mesh, in_specs=placed, out_specs=P("hist", "sess", None, None), check_vma=False
    )
```

```python
import functools

import jax
import jax.numpy as jnp
from jax import lax
from jax.experimental import pallas as pl
from jax.experimental.pallas import tpu as pltpu
from jax.sharding import PartitionSpec as P

HEADS = 16
SPP = 32
LONGEST = 48
QUERIES = 64
PARTS = 6
BF16 = jnp.bfloat16
F32 = jnp.float32
NT = (((1,), (1,)), ((), ()))
TN = (((0,), (0,)), ((), ()))


def iota(shape, dim):
    return lax.broadcasted_iota(jnp.int32, shape, dim)


def mm(a, b, dims=(((1,), (0,)), ((), ()))):
    return lax.dot_general(a, b, dims, preferred_element_type=F32)


def split(x):
    high = x.astype(BF16)
    return high, (x - high.astype(F32)).astype(BF16)


def mm3(a, b, dims=(((1,), (0,)), ((), ()))):
    a_high, a_low = split(a)
    b_high, b_low = split(b)
    return mm(a_high, b_high, dims) + (mm(a_low, b_high, dims) + mm(a_high, b_low, dims))


def same_head(columns):
    shape = (columns, columns)
    return (iota(shape, 0) // 64 == iota(shape, 1) // 64).astype(F32).astype(BF16)


def slots_of(owner_row, users):
    owned = owner_row == iota((users, SPP), 0)
    earlier = (iota((SPP, SPP), 0) < iota((SPP, SPP), 1)).astype(BF16)
    before = mm(owned.astype(F32).astype(BF16), earlier)
    return [(owned & (before == float(rank))).astype(F32) for rank in range(2)]


def windows(length):
    result = []
    for start in range(0, length, QUERIES):
        low, high = max(0, start - LONGEST), min(length, start + QUERIES + LONGEST)
        result.append((start, low, high - low))
    return result


def encode_kernel(
    users,
    groups,
    events_hbm,
    w_hbm,
    pattern_hbm,
    owner_hbm,
    gap_hbm,
    rates_hbm,
    send_hbm,
    keep_hbm,
    send_ref,
    keep_ref,
    fade_ref,
    rows_ref,
    w_ref,
    pattern_ref,
    owner_ref,
    gap_ref,
    rates_ref,
    mask_ref,
    query_ref,
    key_ref,
    value_ref,
    weight_ref,
    small_sem,
    events_sem,
    w_sem,
    out_sem,
):
    length, width = events_hbm.shape
    columns = 256
    here = columns // 64
    steps = width // columns
    subs = columns // 128
    chunk = subs * users * PARTS
    small = [
        pltpu.make_async_copy(source, target, small_sem.at[n])
        for n, (source, target) in enumerate(
            [
                (pattern_hbm, pattern_ref),
                (owner_hbm, owner_ref),
                (gap_hbm, gap_ref),
                (rates_hbm, rates_ref),
            ]
        )
    ]
    in_events = pltpu.make_async_copy(events_hbm, rows_ref.at[0:length], events_sem)
    in_w = [
        [
            pltpu.make_async_copy(
                w_hbm.at[:, part * width + step * columns : part * width + (step + 1) * columns],
                w_ref.at[step * 3 + part],
                w_sem.at[step * 3 + part],
            )
            for part in range(3)
        ]
        for step in range(steps)
    ]
    out_keys = pltpu.make_async_copy(
        keep_ref.at[2 * users :], keep_hbm.at[2 * users :], out_sem.at[steps]
    )
    out_queries = pltpu.make_async_copy(
        keep_ref.at[0 : 2 * users], keep_hbm.at[0 : 2 * users], out_sem.at[steps + 1]
    )
    out = [
        pltpu.make_async_copy(
            send_ref.at[step * chunk : (step + 1) * chunk],
            send_hbm.at[step * chunk : (step + 1) * chunk],
            out_sem.at[step],
        )
        for step in range(steps)
    ]
    for copy in small:
        copy.start()
    in_events.start()
    for copy in in_w[0]:
        copy.start()
    for copy in small:
        copy.wait()

    pattern = pattern_ref[...]
    members = (pattern == iota((SPP, length), 0)).astype(F32).astype(BF16)
    slots = slots_of(owner_ref[...], users)
    place = mm(jnp.concatenate(slots, axis=0).astype(BF16), members)
    counts = jnp.sum(place, axis=1, keepdims=True)
    place = place.astype(BF16)
    inverse = jnp.broadcast_to(1.0 / jnp.maximum(counts, 1.0), (2 * users, columns))
    ids = iota((SPP, 128), 0).astype(F32).astype(BF16)
    id_column = mm(members, ids, TN)
    id_row = pattern.astype(F32)
    offset = 0
    for start, low, size in windows(length):
        block = id_row[:, start : start + QUERIES]
        same = id_column[low : low + size] == jnp.concatenate([block, block], axis=1)
        mask_ref[offset : offset + size, :] = jnp.where(same, 0.0, -jnp.inf)
        offset += size
    gap_row = gap_ref[...].astype(F32)
    gaps = [jnp.sum(slot * gap_row, axis=1, keepdims=True) for slot in slots]
    lane = iota((1, 128), 1)
    first = lane < 64
    for group in range(groups):
        at = slice(group * 128, (group + 1) * 128)
        rate = jnp.where(first, rates_ref[2 * group], rates_ref[2 * group + 1])
        fade_ref[0:users, at] = jnp.exp(-rate * gaps[0])
        fade_ref[users:, at] = jnp.exp(-rate * (gaps[0] + gaps[1]))
        keep_ref[6 * users :, at] = jnp.exp(-rate * gaps[1])

    head_of = iota((1, columns), 1) // 64
    only = [jnp.where(head_of == head, 0.125, 0.0).astype(BF16) for head in range(here)]
    spread = same_head(columns)

    def put(group, part, rows):
        for rank in range(2):
            send_ref[pl.ds(group * users * PARTS + part * 2 + rank, users, stride=PARTS), :] = rows[
                rank
            ]

    def project(step):
        for part, target in enumerate((query_ref, key_ref, value_ref)):
            for at in range(0, length, 256):
                rows = rows_ref[at : at + 256, :]
                target[step, at : at + 256, :] = mm(rows, w_ref[step * 3 + part]).astype(BF16)

    def average(step):
        means = []
        for part in (1, 2):
            both = mm(rows_ref[length:, :], w_ref[step * 3 + part])
            mean = (both[: 2 * users] + both[2 * users :]) * inverse
            keep_ref[
                2 * part * users : 2 * (part + 1) * users, step * columns : (step + 1) * columns
            ] = mean
            means.append(mean)
        for sub in range(subs):
            group = step * subs + sub
            key, later_key, value, later_value = [
                mean[rank * users : (rank + 1) * users, sub * 128 : (sub + 1) * 128]
                for mean in means
                for rank in range(2)
            ]
            key = key * keep_ref[6 * users :, group * 128 : (group + 1) * 128]
            x, y = key[:, 0:1], later_key[:, 0:1]
            size = jnp.maximum(jnp.abs(x), jnp.abs(y))
            some = size > 0.0
            size = jnp.where(some, size, 1.0)
            x, y = jnp.where(some, x / size, 1.0), y / size
            norm = jnp.sqrt(x * x + y * y)
            cosine = jnp.where(first, x / norm, 1.0)
            sine = jnp.where(first, y / norm, 0.0)
            turned = cosine * later_key - sine * key
            total = gaps[0] + gaps[1]
            put(group, 1, (cosine * key + sine * later_key, jnp.where(lane == 0, total, turned)))
            put(
                group,
                2,
                (cosine * value + sine * later_value, cosine * later_value - sine * value),
            )

    def attend(step):
        offset = 0
        reached = 0
        for start, low, size in windows(length):
            block = query_ref[step, start : start + QUERIES, :]
            stacked = jnp.concatenate([block * keep for keep in only], axis=0)
            scores = mm(key_ref[step, low : low + size, :], stacked, NT)
            mask = mask_ref[offset : offset + size, :]
            offset += size
            probs = []
            for half in range(columns // 128):
                part = scores[:, half * 128 : (half + 1) * 128] + mask
                expd = jnp.exp(part - jnp.max(part, axis=0, keepdims=True))
                probs.append(expd * (1.0 / jnp.sum(expd, axis=0, keepdims=True)))
            probs = jnp.concatenate(probs, axis=1)
            known = reached - low
            if known:
                weight_ref[step, low:reached, :] += probs[:known]
            weight_ref[step, reached : low + size, :] = probs[known:]
            reached = low + size

    def finish(step):
        weight = mm(weight_ref[step].astype(BF16), spread)
        high, low = split(weight * value_ref[step].astype(F32))
        mean = (mm(place, high) + mm(place, low)) * inverse
        keep_ref[0 : 2 * users, step * columns : (step + 1) * columns] = mean
        for sub in range(subs):
            group = step * subs + sub
            faded = mean[:, sub * 128 : (sub + 1) * 128] * fade_ref[
                :, group * 128 : (group + 1) * 128
            ]
            put(group, 0, (faded[:users], faded[users:]))

    in_events.wait()
    for copies in in_w[1:]:
        for copy in copies:
            copy.start()
    for copy in in_w[0]:
        copy.wait()
    high, low = split(mm(place, rows_ref[0:length, :]))
    rows_ref[length : length + 2 * users, :] = high
    rows_ref[length + 2 * users :, :] = low
    project(0)
    for copies in in_w[1:2]:
        for copy in copies:
            copy.wait()
    project(1)
    for copies in in_w[2:4]:
        for copy in copies:
            copy.wait()
    project(2)
    attend(0)
    project(3)
    attend(1)
    average(0)
    average(1)
    average(2)
    average(3)
    attend(2)
    finish(0)
    finish(1)
    out_keys.start()
    out[0].start()
    out[1].start()
    attend(3)
    finish(2)
    finish(3)
    out_queries.start()
    out[2].start()
    out[3].start()
    for copy in [out_keys, out_queries] + out:
        copy.wait()


def encode(events, w_qkv, patterns, owners, gaps, rates, users, groups):
    length, width = events.shape
    columns = 256
    steps = width // columns
    window_rows = sum(size for _, _, size in windows(length))
    send = jax.ShapeDtypeStruct((groups * users * PARTS, 128), F32)
    keep = jax.ShapeDtypeStruct((7 * users, width), F32)
    return pl.pallas_call(
        functools.partial(encode_kernel, users, groups),
        in_specs=[pl.BlockSpec(memory_space=pl.ANY)] * 6,
        out_specs=[pl.BlockSpec(memory_space=pl.ANY)] * 2,
        out_shape=[send, keep],
        scratch_shapes=[
            pltpu.VMEM(send.shape, F32),
            pltpu.VMEM(keep.shape, F32),
            pltpu.VMEM((2 * users, width), F32),
            pltpu.VMEM((length + 4 * users, width), BF16),
            pltpu.VMEM((3 * steps, width, columns), BF16),
            pltpu.VMEM((1, length), jnp.int32),
            pltpu.VMEM((1, SPP), jnp.int32),
            pltpu.VMEM((1, SPP), jnp.int32),
            pltpu.SMEM(rates.shape, F32),
            pltpu.VMEM((window_rows, 128), F32),
            pltpu.VMEM((steps, length, columns), BF16),
            pltpu.VMEM((steps, length, columns), BF16),
            pltpu.VMEM((steps, length, columns), BF16),
            pltpu.VMEM((steps, length, columns), F32),
            pltpu.SemaphoreType.DMA((4,)),
            pltpu.SemaphoreType.DMA,
            pltpu.SemaphoreType.DMA((3 * steps,)),
            pltpu.SemaphoreType.DMA((steps + 2,)),
        ],
        compiler_params=pltpu.CompilerParams(vmem_limit_bytes=60 * 1024 * 1024),
        name="encode",
    )(events, w_qkv, patterns, owners, gaps, rates)


def within_kernel(users, keep_ref, out_ref):
    query, later_query, key, later_key, value, later_value, fade = [
        keep_ref[n * users : (n + 1) * users, :] for n in range(7)
    ]
    products = jnp.concatenate([query * key, later_query * key, later_query * later_key], axis=0)
    columns = 256
    spread = same_head(columns)
    for at in range(0, products.shape[1], columns):
        here = slice(at, at + columns)
        part = products[:, here]
        high = part.astype(BF16)
        middle, low = split(part - high.astype(F32))
        dots = mm(high, spread) + (mm(middle, spread) + mm(low, spread))
        out_ref[:users, here] = dots[:users] * value[:, here]
        out_ref[users:, here] = (
            fade[:, here] * dots[users : 2 * users] * value[:, here]
            + dots[2 * users :] * later_value[:, here]
        )


def within(keep, users):
    width = keep.shape[1]
    return pl.pallas_call(
        functools.partial(within_kernel, users),
        out_shape=jax.ShapeDtypeStruct((2 * users, width), F32),
        compiler_params=pltpu.CompilerParams(vmem_limit_bytes=16 * 1024 * 1024),
        cost_estimate=pl.CostEstimate(
            flops=2 * 9 * users * width * 256, bytes_accessed=9 * users * width * 4, transcendentals=0
        ),
        name="within",
    )(keep)


def recur_kernel(packs, rates_hbm, rows_ref, prior_hbm, out_ref, rates_ref, prior_ref, sem):
    group = lax.axis_index("hist")
    in_rates = pltpu.make_async_copy(rates_hbm, rates_ref, sem.at[0])
    in_prior = pltpu.make_async_copy(prior_hbm.at[pl.ds(2 * group, 2)], prior_ref, sem.at[1])
    in_rates.start()
    in_prior.start()
    half = packs // 2
    load = lambda part, late: rows_ref[pl.ds(late * half * PARTS + part, half, stride=PARTS), :]
    both = lambda part: [load(part + rank, late) for late in range(2) for rank in range(2)]
    lane = iota((1, 128), 1)
    first = lane < 64

    keys = both(2)
    gap = jnp.concatenate([jnp.broadcast_to(keys[n][:, 0:1], (half, 128)) for n in (1, 3)], axis=0)
    reached = (iota((packs, packs), 0) >= iota((packs, packs), 1)).astype(F32).astype(BF16)
    ended = mm(reached, gap.astype(BF16))
    started = ended - gap
    ended_row = ended.T[0:1, :]
    earlier = iota((half, half), 0) > iota((half, half), 1)
    since = {}
    for late in range(2):
        for source in range(late + 1):
            gone = started[late * half : (late + 1) * half] - ended_row[:, source * half : (source + 1) * half]
            since[late, source] = jnp.where(earlier, gone, 1e30) if late == source else gone

    keys = [jnp.where(lane == 0, 0.0, rows) if n % 2 else rows for n, rows in enumerate(keys)]
    query, key, value = [jnp.concatenate(rows, axis=0) for rows in (both(0), keys, both(4))]
    turned_query, turned_key = pltpu.roll(query, 64, 1), pltpu.roll(key, 64, 1)
    value_high, value_low = split(value)
    value_both = jnp.concatenate([value_high, value_low], axis=1)
    in_rates.wait()
    in_prior.wait()
    rate = [rates_ref[2 * group], rates_ref[2 * group + 1]]

    def pieces(x):
        high = x.astype(BF16).astype(F32)
        return high, x - high

    sides = []
    for head in range(2):
        mine = first if head == 0 else jnp.logical_not(first)
        q_high, q_low = pieces(jnp.where(mine, query, turned_query))
        k_high, k_low = pieces(jnp.where(mine, key, turned_key))
        left = jnp.concatenate(
            [jnp.where(first, q_high, q_low), jnp.where(first, q_high, 0.0)], axis=1
        )
        right = jnp.concatenate([k_high, jnp.where(first, k_low, 0.0)], axis=1)
        sides.append((left.astype(BF16), right.astype(BF16)))

    empty = jnp.zeros((64, 64), F32)
    prior = jnp.concatenate(
        [
            jnp.concatenate([prior_ref[0], empty], axis=1),
            jnp.concatenate([empty, prior_ref[1]], axis=1),
        ],
        axis=0,
    )
    prior_high, prior_low = split(prior)
    prior_twice = jnp.concatenate([prior_high, prior_high], axis=0)
    lane_rate = jnp.where(first, rate[0], rate[1])

    for late in range(2):
        mine = slice(late * packs, (late + 1) * packs)
        seen = slice(0, (late + 1) * packs)
        heads = []
        for head in range(2):
            left, right = sides[head]
            fades = []
            for source in range(late + 1):
                fades += [jnp.exp(-rate[head] * since[late, source])] * 2
            fades = jnp.concatenate(fades, axis=1)
            scores = mm(left[mine], right[seen], NT) * jnp.concatenate([fades, fades], axis=0)
            s_high, s_low = split(scores)
            wide = mm(s_high, value_both[seen])
            heads.append(wide[:, :128] + (wide[:, 128:] + mm(s_low, value_high[seen])))
        fade = jnp.exp(-lane_rate * started[late * half : (late + 1) * half])
        f_high, f_low = split(query[mine] * jnp.concatenate([fade, fade], axis=0))
        carried = mm(jnp.concatenate([f_high, f_low], axis=1), prior_twice) + mm(f_high, prior_low)
        result = jnp.where(first, heads[0], heads[1]) + carried
        for rank in range(2):
            out_ref[pl.ds(late * packs + rank, half, stride=2), :] = (
                result[rank * half : (rank + 1) * half]
            )


def recur(rates, rows, prior, packs):
    return pl.pallas_call(
        functools.partial(recur_kernel, packs),
        in_specs=[
            pl.BlockSpec(memory_space=pl.ANY),
            pl.BlockSpec(memory_space=pltpu.VMEM),
            pl.BlockSpec(memory_space=pl.ANY),
        ],
        out_shape=jax.ShapeDtypeStruct((2 * packs, 128), F32),
        scratch_shapes=[
            pltpu.SMEM(rates.shape, F32),
            pltpu.VMEM((2, 64, 64), F32),
            pltpu.SemaphoreType.DMA((2,)),
        ],
        compiler_params=pltpu.CompilerParams(vmem_limit_bytes=40 * 1024 * 1024),
        name="recur",
    )(rates, rows, prior)


def pick_kernel(users, groups, owner_hbm, rows_ref, within_ref, out_ref, owner_ref, sem):
    in_owner = pltpu.make_async_copy(owner_hbm, owner_ref, sem)
    in_owner.start()
    in_owner.wait()
    slots = jnp.concatenate(slots_of(owner_ref[...], users), axis=0).astype(BF16)
    mine = within_ref[...] + jnp.concatenate(
        [
            jnp.concatenate(
                [
                    rows_ref[pl.ds(group * users * 2 + rank, users, stride=2), :]
                    for rank in range(2)
                ],
                axis=0,
            )
            for group in range(groups)
        ],
        axis=1,
    )
    high = mine.astype(BF16)
    middle, low = split(mine - high.astype(F32))
    out_ref[...] = mm(slots, high, TN) + (mm(slots, middle, TN) + mm(slots, low, TN))


def pick(owners, rows, inside, users, groups):
    return pl.pallas_call(
        functools.partial(pick_kernel, users, groups),
        in_specs=[
            pl.BlockSpec(memory_space=pl.ANY),
            pl.BlockSpec(memory_space=pltpu.VMEM),
            pl.BlockSpec(memory_space=pltpu.VMEM),
        ],
        out_shape=jax.ShapeDtypeStruct((SPP, groups * 128), F32),
        scratch_shapes=[pltpu.VMEM((1, SPP), jnp.int32), pltpu.SemaphoreType.DMA],
        compiler_params=pltpu.CompilerParams(vmem_limit_bytes=16 * 1024 * 1024),
        name="pick",
    )(owners, rows, inside)


def shards(events, w_qkv, patterns, owners, gaps, rates, prior_state):
    groups = lax.axis_size("hist")
    users = lax.axis_size("sess")
    packs = groups * users
    axes = ("hist", "sess")
    send, keep = encode(
        events[0, 0], w_qkv, patterns[0], owners[0], gaps[0], rates, users, groups
    )
    arrived = lax.all_to_all(
        send.reshape(packs, PARTS, 1, 128), axes, split_axis=0, concat_axis=0, tiled=True
    ).reshape(packs * PARTS, 128)
    inside = within(keep, users)
    arrived, inside = lax.optimization_barrier((arrived, inside))
    done = recur(rates, arrived, prior_state[0], packs)
    returned = lax.all_to_all(
        done.reshape(packs, 2, 128), axes, split_axis=0, concat_axis=0, tiled=True
    ).reshape(packs * 2, 128)
    return pick(owners[0], returned, inside, users, groups)[None, None]


def solution(mesh):
    placed = (
        P("hist", "sess", None, None),
        P(),
        P("hist", "sess", None),
        P("hist", "sess", None),
        P("hist", "sess", None),
        P(),
        P("sess", None, None, None),
    )
    return jax.shard_map(
        shards, mesh=mesh, in_specs=placed, out_specs=P("hist", "sess", None, None), check_vma=False
    )
```

```python
import functools

import jax
import jax.numpy as jnp
from jax import lax
from jax.experimental import pallas as pl
from jax.experimental.pallas import tpu as pltpu
from jax.sharding import PartitionSpec as P

HEADS = 16
SPP = 32
LONGEST = 48
QUERIES = 64
PARTS = 6
BF16 = jnp.bfloat16
F32 = jnp.float32
NT = (((1,), (1,)), ((), ()))
TN = (((0,), (0,)), ((), ()))


def iota(shape, dim):
    return lax.broadcasted_iota(jnp.int32, shape, dim)


def mm(a, b, dims=(((1,), (0,)), ((), ()))):
    return lax.dot_general(a, b, dims, preferred_element_type=F32)


def split(x):
    high = x.astype(BF16)
    return high, (x - high.astype(F32)).astype(BF16)


def mm3(a, b, dims=(((1,), (0,)), ((), ()))):
    a_high, a_low = split(a)
    b_high, b_low = split(b)
    return mm(a_high, b_high, dims) + (mm(a_low, b_high, dims) + mm(a_high, b_low, dims))


def same_head(columns):
    shape = (columns, columns)
    return (iota(shape, 0) // 64 == iota(shape, 1) // 64).astype(F32).astype(BF16)


def slots_of(owner_row, users):
    owned = owner_row == iota((users, SPP), 0)
    earlier = (iota((SPP, SPP), 0) < iota((SPP, SPP), 1)).astype(BF16)
    before = mm(owned.astype(F32).astype(BF16), earlier)
    return [(owned & (before == float(rank))).astype(F32) for rank in range(2)]


def windows(length):
    result = []
    for start in range(0, length, QUERIES):
        low, high = max(0, start - LONGEST), min(length, start + QUERIES + LONGEST)
        result.append((start, low, high - low))
    return result


def encode_kernel(
    users,
    groups,
    events_hbm,
    w_hbm,
    pattern_hbm,
    owner_hbm,
    gap_hbm,
    rates_hbm,
    send_hbm,
    keep_hbm,
    send_ref,
    keep_ref,
    fade_ref,
    rows_ref,
    w_ref,
    pattern_ref,
    owner_ref,
    gap_ref,
    rates_ref,
    mask_ref,
    query_ref,
    key_ref,
    value_ref,
    weight_ref,
    small_sem,
    events_sem,
    w_sem,
    out_sem,
):
    length, width = events_hbm.shape
    columns = 256
    here = columns // 64
    steps = width // columns
    subs = columns // 128
    chunk = subs * users * PARTS
    small = [
        pltpu.make_async_copy(source, target, small_sem.at[n])
        for n, (source, target) in enumerate(
            [
                (pattern_hbm, pattern_ref),
                (owner_hbm, owner_ref),
                (gap_hbm, gap_ref),
                (rates_hbm, rates_ref),
            ]
        )
    ]
    in_events = pltpu.make_async_copy(events_hbm, rows_ref.at[0:length], events_sem)
    in_w = [
        [
            pltpu.make_async_copy(
                w_hbm.at[:, part * width + step * columns : part * width + (step + 1) * columns],
                w_ref.at[step * 3 + part],
                w_sem.at[step * 3 + part],
            )
            for part in range(3)
        ]
        for step in range(steps)
    ]
    out_keys = pltpu.make_async_copy(
        keep_ref.at[2 * users :], keep_hbm.at[2 * users :], out_sem.at[steps]
    )
    out_queries = pltpu.make_async_copy(
        keep_ref.at[0 : 2 * users], keep_hbm.at[0 : 2 * users], out_sem.at[steps + 1]
    )
    out = [
        pltpu.make_async_copy(
            send_ref.at[step * chunk : (step + 1) * chunk],
            send_hbm.at[step * chunk : (step + 1) * chunk],
            out_sem.at[step],
        )
        for step in range(steps)
    ]
    for copy in small:
        copy.start()
    in_events.start()
    for copy in in_w[0]:
        copy.start()
    for copy in small:
        copy.wait()

    pattern = pattern_ref[...]
    members = (pattern == iota((SPP, length), 0)).astype(F32).astype(BF16)
    slots = slots_of(owner_ref[...], users)
    place = mm(jnp.concatenate(slots, axis=0).astype(BF16), members)
    counts = jnp.sum(place, axis=1, keepdims=True)
    place = place.astype(BF16)
    inverse = jnp.broadcast_to(1.0 / jnp.maximum(counts, 1.0), (2 * users, columns))
    for copies in in_w[1:4]:
        for copy in copies:
            copy.start()
    ids = iota((SPP, 128), 0).astype(F32).astype(BF16)
    id_column = mm(members, ids, TN)
    id_row = pattern.astype(F32)
    offset = 0
    for start, low, size in windows(length):
        block = id_row[:, start : start + QUERIES]
        same = id_column[low : low + size] == jnp.concatenate([block, block], axis=1)
        mask_ref[offset : offset + size, :] = jnp.where(same, 0.0, -jnp.inf)
        offset += size
    gap_row = gap_ref[...].astype(F32)
    gaps = [jnp.sum(slot * gap_row, axis=1, keepdims=True) for slot in slots]
    lane = iota((1, 128), 1)
    first = lane < 64
    for group in range(groups):
        at = slice(group * 128, (group + 1) * 128)
        rate = jnp.where(first, rates_ref[2 * group], rates_ref[2 * group + 1])
        fade_ref[0:users, at] = jnp.exp(-rate * gaps[0])
        fade_ref[users:, at] = jnp.exp(-rate * (gaps[0] + gaps[1]))
        keep_ref[6 * users :, at] = jnp.exp(-rate * gaps[1])

    head_of = iota((1, columns), 1) // 64
    only = [jnp.where(head_of == head, 0.125, 0.0).astype(BF16) for head in range(here)]
    spread = same_head(columns)

    def put(group, part, rows):
        for rank in range(2):
            send_ref[pl.ds(group * users * PARTS + part * 2 + rank, users, stride=PARTS), :] = rows[
                rank
            ]

    def project(step):
        for part, target in enumerate((query_ref, key_ref, value_ref)):
            for at in range(0, length, 256):
                rows = rows_ref[at : at + 256, :]
                target[step, at : at + 256, :] = mm(rows, w_ref[step * 3 + part]).astype(BF16)

    def average(step):
        means = []
        for part in (1, 2):
            both = mm(rows_ref[length:, :], w_ref[step * 3 + part])
            mean = (both[: 2 * users] + both[2 * users :]) * inverse
            keep_ref[
                2 * part * users : 2 * (part + 1) * users, step * columns : (step + 1) * columns
            ] = mean
            means.append(mean)
        for sub in range(subs):
            group = step * subs + sub
            key, later_key, value, later_value = [
                mean[rank * users : (rank + 1) * users, sub * 128 : (sub + 1) * 128]
                for mean in means
                for rank in range(2)
            ]
            key = key * keep_ref[6 * users :, group * 128 : (group + 1) * 128]
            x, y = key[:, 0:1], later_key[:, 0:1]
            size = jnp.maximum(jnp.abs(x), jnp.abs(y))
            some = size > 0.0
            size = jnp.where(some, size, 1.0)
            x, y = jnp.where(some, x / size, 1.0), y / size
            norm = jnp.sqrt(x * x + y * y)
            cosine = jnp.where(first, x / norm, 1.0)
            sine = jnp.where(first, y / norm, 0.0)
            turned = cosine * later_key - sine * key
            total = gaps[0] + gaps[1]
            put(group, 1, (cosine * key + sine * later_key, jnp.where(lane == 0, total, turned)))
            put(
                group,
                2,
                (cosine * value + sine * later_value, cosine * later_value - sine * value),
            )

    def attend(step):
        offset = 0
        reached = 0
        for start, low, size in windows(length):
            block = query_ref[step, start : start + QUERIES, :]
            stacked = jnp.concatenate([block * keep for keep in only], axis=0)
            scores = mm(key_ref[step, low : low + size, :], stacked, NT)
            mask = mask_ref[offset : offset + size, :]
            offset += size
            probs = []
            for half in range(columns // 128):
                part = scores[:, half * 128 : (half + 1) * 128] + mask
                expd = jnp.exp(part - jnp.max(part, axis=0, keepdims=True))
                probs.append(expd * (1.0 / jnp.sum(expd, axis=0, keepdims=True)))
            probs = jnp.concatenate(probs, axis=1)
            known = reached - low
            if known:
                weight_ref[step, low:reached, :] += probs[:known]
            weight_ref[step, reached : low + size, :] = probs[known:]
            reached = low + size

    def finish(step):
        mean = None
        for at in range(0, length, 128):
            weight = mm(weight_ref[step, at : at + 128, :].astype(BF16), spread)
            high, low = split(weight * value_ref[step, at : at + 128, :].astype(F32))
            some = mm(place[:, at : at + 128], high) + mm(place[:, at : at + 128], low)
            mean = some if mean is None else mean + some
        mean = mean * inverse
        keep_ref[0 : 2 * users, step * columns : (step + 1) * columns] = mean
        for sub in range(subs):
            group = step * subs + sub
            faded = mean[:, sub * 128 : (sub + 1) * 128] * fade_ref[
                :, group * 128 : (group + 1) * 128
            ]
            put(group, 0, (faded[:users], faded[users:]))

    in_events.wait()
    for copy in in_w[0]:
        copy.wait()
    high, low = split(mm(place, rows_ref[0:length, :]))
    rows_ref[length : length + 2 * users, :] = high
    rows_ref[length + 2 * users :, :] = low
    project(0)
    for copies in in_w[1:2]:
        for copy in copies:
            copy.wait()
    project(1)
    for copies in in_w[2:4]:
        for copy in copies:
            copy.wait()
    attend(0)
    average(0)
    attend(1)
    average(1)
    project(2)
    attend(2)
    average(2)
    project(3)
    attend(3)
    average(3)
    finish(0)
    finish(1)
    out_keys.start()
    out[0].start()
    out[1].start()
    finish(2)
    out[2].start()
    finish(3)
    out[3].start()
    out_queries.start()
    for copy in [out_keys, out_queries] + out:
        copy.wait()


def encode(events, w_qkv, patterns, owners, gaps, rates, users, groups):
    length, width = events.shape
    columns = 256
    steps = width // columns
    window_rows = sum(size for _, _, size in windows(length))
    send = jax.ShapeDtypeStruct((groups * users * PARTS, 128), F32)
    keep = jax.ShapeDtypeStruct((7 * users, width), F32)
    return pl.pallas_call(
        functools.partial(encode_kernel, users, groups),
        in_specs=[pl.BlockSpec(memory_space=pl.ANY)] * 6,
        out_specs=[pl.BlockSpec(memory_space=pl.ANY)] * 2,
        out_shape=[send, keep],
        scratch_shapes=[
            pltpu.VMEM(send.shape, F32),
            pltpu.VMEM(keep.shape, F32),
            pltpu.VMEM((2 * users, width), F32),
            pltpu.VMEM((length + 4 * users, width), BF16),
            pltpu.VMEM((3 * steps, width, columns), BF16),
            pltpu.VMEM((1, length), jnp.int32),
            pltpu.VMEM((1, SPP), jnp.int32),
            pltpu.VMEM((1, SPP), jnp.int32),
            pltpu.SMEM(rates.shape, F32),
            pltpu.VMEM((window_rows, 128), F32),
            pltpu.VMEM((steps, length, columns), BF16),
            pltpu.VMEM((steps, length, columns), BF16),
            pltpu.VMEM((steps, length, columns), BF16),
            pltpu.VMEM((steps, length, columns), F32),
            pltpu.SemaphoreType.DMA((4,)),
            pltpu.SemaphoreType.DMA,
            pltpu.SemaphoreType.DMA((3 * steps,)),
            pltpu.SemaphoreType.DMA((steps + 2,)),
        ],
        compiler_params=pltpu.CompilerParams(vmem_limit_bytes=60 * 1024 * 1024),
        name="encode",
    )(events, w_qkv, patterns, owners, gaps, rates)


def within_kernel(users, owner_ref, keep_ref, out_ref, chosen_ref):
    query, later_query, key, later_key, value, later_value, fade = [
        keep_ref[n * users : (n + 1) * users, :] for n in range(7)
    ]
    products = jnp.concatenate([query * key, later_query * key, later_query * later_key], axis=0)
    chosen_ref[...] = jnp.concatenate(slots_of(owner_ref[...], users), axis=0).T
    columns = 256
    spread = same_head(columns)
    for at in range(0, products.shape[1], columns):
        here = slice(at, at + columns)
        part = products[:, here]
        high = part.astype(BF16)
        middle, low = split(part - high.astype(F32))
        dots = mm(high, spread) + (mm(middle, spread) + mm(low, spread))
        out_ref[:users, here] = dots[:users] * value[:, here]
        out_ref[users:, here] = (
            fade[:, here] * dots[users : 2 * users] * value[:, here]
            + dots[2 * users :] * later_value[:, here]
        )


def within(owners, keep, users):
    width = keep.shape[1]
    return pl.pallas_call(
        functools.partial(within_kernel, users),
        out_shape=[
            jax.ShapeDtypeStruct((2 * users, width), F32),
            jax.ShapeDtypeStruct((SPP, 2 * users), F32),
        ],
        compiler_params=pltpu.CompilerParams(vmem_limit_bytes=16 * 1024 * 1024),
        cost_estimate=pl.CostEstimate(
            flops=2 * 9 * users * width * 256, bytes_accessed=9 * users * width * 4, transcendentals=0
        ),
        name="within",
    )(owners, keep)


def recur_kernel(packs, users, rates_hbm, rows_ref, prior_ref, out_ref, rates_ref, sem):
    core = lax.axis_index("core")
    group = 2 * lax.axis_index("chip") + core
    in_rates = pltpu.make_async_copy(rates_hbm, rates_ref, sem)
    in_rates.start()
    half = packs // 2
    load = lambda part, late: rows_ref[pl.ds(late * half * PARTS + part, half, stride=PARTS), :]
    both = lambda part: [load(part + rank, late) for late in range(2) for rank in range(2)]
    lane = iota((1, 128), 1)
    first = lane < 64

    keys = both(2)
    gap = jnp.concatenate([jnp.broadcast_to(keys[n][:, 0:1], (half, 128)) for n in (1, 3)], axis=0)
    reached = (iota((packs, packs), 0) >= iota((packs, packs), 1)).astype(F32).astype(BF16)
    ended = mm(reached, gap.astype(BF16))
    started = ended - gap
    ended_row = ended.T[0:1, :]
    earlier = iota((half, half), 0) > iota((half, half), 1)
    since = {}
    for late in range(2):
        for source in range(late + 1):
            gone = started[late * half : (late + 1) * half] - ended_row[:, source * half : (source + 1) * half]
            since[late, source] = jnp.where(earlier, gone, 1e30) if late == source else gone

    keys = [jnp.where(lane == 0, 0.0, rows) if n % 2 else rows for n, rows in enumerate(keys)]
    query, key, value = [jnp.concatenate(rows, axis=0) for rows in (both(0), keys, both(4))]
    turned_query, turned_key = pltpu.roll(query, 64, 1), pltpu.roll(key, 64, 1)
    value_high, value_low = split(value)
    value_both = jnp.concatenate([value_high, value_low], axis=1)
    in_rates.wait()
    rate = [rates_ref[2 * group], rates_ref[2 * group + 1]]

    def pieces(x):
        high = x.astype(BF16).astype(F32)
        return high, x - high

    sides = []
    for head in range(2):
        mine = first if head == 0 else jnp.logical_not(first)
        q_high, q_low = pieces(jnp.where(mine, query, turned_query))
        k_high, k_low = pieces(jnp.where(mine, key, turned_key))
        left = jnp.concatenate(
            [jnp.where(first, q_high, q_low), jnp.where(first, q_high, 0.0)], axis=1
        )
        right = jnp.concatenate([k_high, jnp.where(first, k_low, 0.0)], axis=1)
        sides.append((left.astype(BF16), right.astype(BF16)))

    empty = jnp.zeros((64, 64), F32)
    prior = jnp.concatenate(
        [
            jnp.concatenate([prior_ref[2 * group], empty], axis=1),
            jnp.concatenate([empty, prior_ref[2 * group + 1]], axis=1),
        ],
        axis=0,
    )
    prior_high, prior_low = split(prior)
    prior_twice = jnp.concatenate([prior_high, prior_high], axis=0)
    lane_rate = jnp.where(first, rate[0], rate[1])

    for late in range(2):
        mine = slice(late * packs, (late + 1) * packs)
        seen = slice(0, (late + 1) * packs)
        heads = []
        for head in range(2):
            left, right = sides[head]
            fades = []
            for source in range(late + 1):
                fades += [jnp.exp(-rate[head] * since[late, source])] * 2
            fades = jnp.concatenate(fades, axis=1)
            scores = mm(left[mine], right[seen], NT) * jnp.concatenate([fades, fades], axis=0)
            s_high, s_low = split(scores)
            wide = mm(s_high, value_both[seen])
            heads.append(wide[:, :128] + (wide[:, 128:] + mm(s_low, value_high[seen])))
        fade = jnp.exp(-lane_rate * started[late * half : (late + 1) * half])
        f_high, f_low = split(query[mine] * jnp.concatenate([fade, fade], axis=0))
        carried = mm(jnp.concatenate([f_high, f_low], axis=1), prior_twice) + mm(f_high, prior_low)
        result = jnp.where(first, heads[0], heads[1]) + carried
        for at in range(0, half, users):
            segment = (late * half + at) // users
            other = core if segment % 2 == 0 else 1 - core
            for rank in range(2):
                row = segment // 2 * users * 4 + 2 * other + rank
                out_ref[pl.ds(row, users, stride=4), :] = result[
                    rank * half + at : rank * half + at + users
                ]


def recur(rates, rows, prior, packs, users):
    return pl.pallas_call(
        functools.partial(recur_kernel, packs, users),
        in_specs=[
            pl.BlockSpec(memory_space=pl.ANY),
            pl.BlockSpec(memory_space=pltpu.VMEM),
            pl.BlockSpec(memory_space=pltpu.VMEM),
        ],
        out_shape=jax.ShapeDtypeStruct((2 * packs, 128), F32),
        scratch_shapes=[pltpu.SMEM(rates.shape, F32), pltpu.SemaphoreType.DMA],
        compiler_params=pltpu.CompilerParams(vmem_limit_bytes=40 * 1024 * 1024),
        name="recur",
    )(rates, rows, prior)


def pick_kernel(users, groups, chosen_ref, rows_ref, other_ref, within_ref, out_ref):
    core = lax.axis_index("core")
    chosen = chosen_ref[...].astype(BF16)
    mine = []
    for group in range(groups):
        chip = group // 2 * users
        here = [rows_ref[pl.ds(chip * 4 + rank, users, stride=4), :] for rank in range(2)]
        there = [other_ref[pl.ds(chip * 2 + rank, users, stride=2), :] for rank in range(2)]
        here, there = [jnp.concatenate(rows, axis=0) for rows in (here, there)]
        mine.append(jnp.where(core == group % 2, here, there))
    mine = within_ref[...] + jnp.concatenate(mine, axis=1)
    high = mine.astype(BF16)
    middle, low = split(mine - high.astype(F32))
    out_ref[...] = mm(chosen, high) + (mm(chosen, middle) + mm(chosen, low))


def pick(chosen, rows, other, inside, users, groups):
    return pl.pallas_call(
        functools.partial(pick_kernel, users, groups),
        in_specs=[pl.BlockSpec(memory_space=pltpu.VMEM)] * 4,
        out_shape=jax.ShapeDtypeStruct((SPP, groups * 128), F32),
        compiler_params=pltpu.CompilerParams(vmem_limit_bytes=16 * 1024 * 1024),
        name="pick",
    )(chosen, rows, other, inside)


def shards(events, w_qkv, patterns, owners, gaps, rates, prior_state):
    chips = lax.axis_size("chip")
    groups = 2 * chips
    users = lax.axis_size("sess")
    packs = groups * users
    send, keep = encode(
        events[0, 0], w_qkv, patterns[0], owners[0], gaps[0], rates, users, groups
    )
    arrived = lax.all_to_all(
        send.reshape(packs, PARTS, 1, 128),
        ("chip", "core", "sess"),
        split_axis=0,
        concat_axis=0,
        tiled=True,
    ).reshape(packs * PARTS, 128)
    inside, chosen = within(owners[0], keep, users)
    arrived, inside, chosen = lax.optimization_barrier((arrived, inside, chosen))
    done = recur(rates, arrived, prior_state[0], packs, users)
    returned = lax.all_to_all(
        done.reshape(chips * users, 4, 128), ("chip", "sess"), split_axis=0, concat_axis=0, tiled=True
    )
    other = lax.ppermute(returned[:, 2:], "core", [(0, 1), (1, 0)])
    return pick(
        chosen,
        returned.reshape(packs * 2, 128),
        other.reshape(packs, 128),
        inside,
        users,
        groups,
    )[None, None]


def solution(mesh):
    sess, hist = mesh.shape["sess"], mesh.shape["hist"]
    devices = mesh.devices if mesh.axis_names[0] == "sess" else mesh.devices.T
    split_mesh = jax.sharding.Mesh(devices.reshape(sess, hist // 2, 2), ("sess", "chip", "core"))
    segment = ("chip", "core")
    placed = (
        P(segment, "sess", None, None),
        P(),
        P(segment, "sess", None),
        P(segment, "sess", None),
        P(segment, "sess", None),
        P(),
        P("sess", None, None, None),
    )
    return jax.shard_map(
        shards,
        mesh=split_mesh,
        in_specs=placed,
        out_specs=P(segment, "sess", None, None),
        check_vma=False,
    )
```

```python
import functools

import jax
import jax.numpy as jnp
from jax import lax
from jax.experimental import pallas as pl
from jax.experimental.pallas import tpu as pltpu
from jax.sharding import PartitionSpec as P

HEADS = 16
SPP = 32
LONGEST = 48
QUERIES = 64
PARTS = 6
BF16 = jnp.bfloat16
F32 = jnp.float32
NT = (((1,), (1,)), ((), ()))
TN = (((0,), (0,)), ((), ()))


def iota(shape, dim):
    return lax.broadcasted_iota(jnp.int32, shape, dim)


def mm(a, b, dims=(((1,), (0,)), ((), ()))):
    return lax.dot_general(a, b, dims, preferred_element_type=F32)


def split(x):
    high = x.astype(BF16)
    return high, (x - high.astype(F32)).astype(BF16)


def mm3(a, b, dims=(((1,), (0,)), ((), ()))):
    a_high, a_low = split(a)
    b_high, b_low = split(b)
    return mm(a_high, b_high, dims) + (mm(a_low, b_high, dims) + mm(a_high, b_low, dims))


def same_head(columns):
    shape = (columns, columns)
    return (iota(shape, 0) // 64 == iota(shape, 1) // 64).astype(F32).astype(BF16)


def slots_of(owner_row, users):
    owned = owner_row == iota((users, SPP), 0)
    earlier = (iota((SPP, SPP), 0) < iota((SPP, SPP), 1)).astype(BF16)
    before = mm(owned.astype(F32).astype(BF16), earlier)
    return [(owned & (before == float(rank))).astype(F32) for rank in range(2)]


def windows(length):
    result = []
    for start in range(0, length, QUERIES):
        low, high = max(0, start - LONGEST), min(length, start + QUERIES + LONGEST)
        result.append((start, low, high - low))
    return result


def encode_kernel(
    users,
    groups,
    events_hbm,
    w_hbm,
    pattern_hbm,
    owner_hbm,
    gap_hbm,
    rates_hbm,
    send_hbm,
    keep_hbm,
    send_ref,
    keep_ref,
    fade_ref,
    rows_ref,
    w_ref,
    pattern_ref,
    owner_ref,
    gap_ref,
    rates_ref,
    mask_ref,
    query_ref,
    key_ref,
    value_ref,
    weight_ref,
    small_sem,
    events_sem,
    w_sem,
    out_sem,
):
    length, width = events_hbm.shape
    columns = 256
    here = columns // 64
    steps = width // columns
    subs = columns // 128
    chunk = subs * users * PARTS
    small = [
        pltpu.make_async_copy(source, target, small_sem.at[n])
        for n, (source, target) in enumerate(
            [
                (pattern_hbm, pattern_ref),
                (owner_hbm, owner_ref),
                (gap_hbm, gap_ref),
                (rates_hbm, rates_ref),
            ]
        )
    ]
    in_events = pltpu.make_async_copy(events_hbm, rows_ref.at[0:length], events_sem)
    in_w = [
        [
            pltpu.make_async_copy(
                w_hbm.at[:, part * width + step * columns : part * width + (step + 1) * columns],
                w_ref.at[step * 3 + part],
                w_sem.at[step * 3 + part],
            )
            for part in range(3)
        ]
        for step in range(steps)
    ]
    out_keys = pltpu.make_async_copy(
        keep_ref.at[2 * users :], keep_hbm.at[2 * users :], out_sem.at[steps]
    )
    out_queries = pltpu.make_async_copy(
        keep_ref.at[0 : 2 * users], keep_hbm.at[0 : 2 * users], out_sem.at[steps + 1]
    )
    out = [
        pltpu.make_async_copy(
            send_ref.at[step * chunk : (step + 1) * chunk],
            send_hbm.at[step * chunk : (step + 1) * chunk],
            out_sem.at[step],
        )
        for step in range(steps)
    ]
    for copy in small:
        copy.start()
    in_events.start()
    for copy in in_w[0]:
        copy.start()
    for copy in small:
        copy.wait()

    pattern = pattern_ref[...]
    members = (pattern == iota((SPP, length), 0)).astype(F32).astype(BF16)
    slots = slots_of(owner_ref[...], users)
    place = mm(jnp.concatenate(slots, axis=0).astype(BF16), members)
    counts = jnp.sum(place, axis=1, keepdims=True)
    place = place.astype(BF16)
    inverse = jnp.broadcast_to(1.0 / jnp.maximum(counts, 1.0), (2 * users, columns))
    for copies in in_w[1:4]:
        for copy in copies:
            copy.start()
    ids = iota((SPP, 128), 0).astype(F32).astype(BF16)
    id_column = mm(members, ids, TN)
    id_row = pattern.astype(F32)
    offset = 0
    for start, low, size in windows(length):
        block = id_row[:, start : start + QUERIES]
        same = id_column[low : low + size] == jnp.concatenate([block, block], axis=1)
        mask_ref[offset : offset + size, :] = jnp.where(same, 0.0, -jnp.inf)
        offset += size
    gap_row = gap_ref[...].astype(F32)
    gaps = [jnp.sum(slot * gap_row, axis=1, keepdims=True) for slot in slots]
    lane = iota((1, 128), 1)
    first = lane < 64
    for group in range(groups):
        at = slice(group * 128, (group + 1) * 128)
        rate = jnp.where(first, rates_ref[2 * group], rates_ref[2 * group + 1])
        fade_ref[0:users, at] = jnp.exp(-rate * gaps[0])
        fade_ref[users:, at] = jnp.exp(-rate * (gaps[0] + gaps[1]))
        keep_ref[6 * users :, at] = jnp.exp(-rate * gaps[1])

    head_of = iota((1, columns), 1) // 64
    only = [jnp.where(head_of == head, 0.125, 0.0).astype(BF16) for head in range(here)]
    spread = same_head(columns)

    def put(group, part, rows):
        for rank in range(2):
            send_ref[pl.ds(group * users * PARTS + part * 2 + rank, users, stride=PARTS), :] = rows[
                rank
            ]

    def project(step):
        for part, target in enumerate((query_ref, key_ref, value_ref)):
            for at in range(0, length, 256):
                rows = rows_ref[at : at + 256, :]
                target[step, at : at + 256, :] = mm(rows, w_ref[step * 3 + part]).astype(BF16)

    def average(step):
        means = []
        for part in (1, 2):
            both = mm(rows_ref[length:, :], w_ref[step * 3 + part])
            mean = (both[: 2 * users] + both[2 * users :]) * inverse
            keep_ref[
                2 * part * users : 2 * (part + 1) * users, step * columns : (step + 1) * columns
            ] = mean
            means.append(mean)
        for sub in range(subs):
            group = step * subs + sub
            key, later_key, value, later_value = [
                mean[rank * users : (rank + 1) * users, sub * 128 : (sub + 1) * 128]
                for mean in means
                for rank in range(2)
            ]
            key = key * keep_ref[6 * users :, group * 128 : (group + 1) * 128]
            x, y = key[:, 0:1], later_key[:, 0:1]
            size = jnp.maximum(jnp.abs(x), jnp.abs(y))
            some = size > 0.0
            size = jnp.where(some, size, 1.0)
            x, y = jnp.where(some, x / size, 1.0), y / size
            norm = jnp.sqrt(x * x + y * y)
            cosine = jnp.where(first, x / norm, 1.0)
            sine = jnp.where(first, y / norm, 0.0)
            turned = cosine * later_key - sine * key
            total = gaps[0] + gaps[1]
            put(group, 1, (cosine * key + sine * later_key, jnp.where(lane == 0, total, turned)))
            put(
                group,
                2,
                (cosine * value + sine * later_value, cosine * later_value - sine * value),
            )

    def attend(step):
        offset = 0
        reached = 0
        for start, low, size in windows(length):
            block = query_ref[step, start : start + QUERIES, :]
            stacked = jnp.concatenate([block * keep for keep in only], axis=0)
            scores = mm(key_ref[step, low : low + size, :], stacked, NT)
            mask = mask_ref[offset : offset + size, :]
            offset += size
            probs = []
            for half in range(columns // 128):
                part = scores[:, half * 128 : (half + 1) * 128] + mask
                expd = jnp.exp(part - jnp.max(part, axis=0, keepdims=True))
                probs.append(expd * (1.0 / jnp.sum(expd, axis=0, keepdims=True)))
            probs = jnp.concatenate(probs, axis=1)
            known = reached - low
            if known:
                weight_ref[step, low:reached, :] += probs[:known]
            weight_ref[step, reached : low + size, :] = probs[known:]
            reached = low + size

    def finish(step):
        mean = None
        for at in range(0, length, 128):
            weight = mm(weight_ref[step, at : at + 128, :].astype(BF16), spread)
            high, low = split(weight * value_ref[step, at : at + 128, :].astype(F32))
            some = mm(place[:, at : at + 128], high) + mm(place[:, at : at + 128], low)
            mean = some if mean is None else mean + some
        mean = mean * inverse
        keep_ref[0 : 2 * users, step * columns : (step + 1) * columns] = mean
        for sub in range(subs):
            group = step * subs + sub
            faded = mean[:, sub * 128 : (sub + 1) * 128] * fade_ref[
                :, group * 128 : (group + 1) * 128
            ]
            put(group, 0, (faded[:users], faded[users:]))

    in_events.wait()
    for copy in in_w[0]:
        copy.wait()
    high, low = split(mm(place, rows_ref[0:length, :]))
    rows_ref[length : length + 2 * users, :] = high
    rows_ref[length + 2 * users :, :] = low
    project(0)
    for copies in in_w[1:2]:
        for copy in copies:
            copy.wait()
    project(1)
    for copies in in_w[2:4]:
        for copy in copies:
            copy.wait()
    attend(0)
    average(0)
    attend(1)
    average(1)
    project(2)
    attend(2)
    average(2)
    project(3)
    attend(3)
    average(3)
    finish(0)
    finish(1)
    out_keys.start()
    out[0].start()
    out[1].start()
    finish(2)
    out[2].start()
    finish(3)
    out[3].start()
    out_queries.start()
    for copy in [out_keys, out_queries] + out:
        copy.wait()


def encode(events, w_qkv, patterns, owners, gaps, rates, users, groups):
    length, width = events.shape
    columns = 256
    steps = width // columns
    window_rows = sum(size for _, _, size in windows(length))
    send = jax.ShapeDtypeStruct((groups * users * PARTS, 128), F32)
    keep = jax.ShapeDtypeStruct((7 * users, width), F32)
    return pl.pallas_call(
        functools.partial(encode_kernel, users, groups),
        in_specs=[pl.BlockSpec(memory_space=pl.ANY)] * 6,
        out_specs=[pl.BlockSpec(memory_space=pl.ANY)] * 2,
        out_shape=[send, keep],
        scratch_shapes=[
            pltpu.VMEM(send.shape, F32),
            pltpu.VMEM(keep.shape, F32),
            pltpu.VMEM((2 * users, width), F32),
            pltpu.VMEM((length + 4 * users, width), BF16),
            pltpu.VMEM((3 * steps, width, columns), BF16),
            pltpu.VMEM((1, length), jnp.int32),
            pltpu.VMEM((1, SPP), jnp.int32),
            pltpu.VMEM((1, SPP), jnp.int32),
            pltpu.SMEM(rates.shape, F32),
            pltpu.VMEM((window_rows, 128), F32),
            pltpu.VMEM((steps, length, columns), BF16),
            pltpu.VMEM((steps, length, columns), BF16),
            pltpu.VMEM((steps, length, columns), BF16),
            pltpu.VMEM((steps, length, columns), F32),
            pltpu.SemaphoreType.DMA((4,)),
            pltpu.SemaphoreType.DMA,
            pltpu.SemaphoreType.DMA((3 * steps,)),
            pltpu.SemaphoreType.DMA((steps + 2,)),
        ],
        compiler_params=pltpu.CompilerParams(vmem_limit_bytes=60 * 1024 * 1024),
        name="encode",
    )(events, w_qkv, patterns, owners, gaps, rates)


def within_kernel(users, owner_ref, keep_ref, out_ref, chosen_ref):
    query, later_query, key, later_key, value, later_value, fade = [
        keep_ref[n * users : (n + 1) * users, :] for n in range(7)
    ]
    products = jnp.concatenate([query * key, later_query * key, later_query * later_key], axis=0)
    chosen_ref[...] = jnp.concatenate(slots_of(owner_ref[...], users), axis=0).T
    columns = 256
    spread = same_head(columns)
    for at in range(0, products.shape[1], columns):
        here = slice(at, at + columns)
        part = products[:, here]
        high = part.astype(BF16)
        middle, low = split(part - high.astype(F32))
        dots = mm(high, spread) + (mm(middle, spread) + mm(low, spread))
        out_ref[:users, here] = dots[:users] * value[:, here]
        out_ref[users:, here] = (
            fade[:, here] * dots[users : 2 * users] * value[:, here]
            + dots[2 * users :] * later_value[:, here]
        )


def within(owners, keep, users):
    width = keep.shape[1]
    return pl.pallas_call(
        functools.partial(within_kernel, users),
        out_shape=[
            jax.ShapeDtypeStruct((2 * users, width), F32),
            jax.ShapeDtypeStruct((SPP, 2 * users), F32),
        ],
        compiler_params=pltpu.CompilerParams(vmem_limit_bytes=16 * 1024 * 1024),
        cost_estimate=pl.CostEstimate(
            flops=2 * 9 * users * width * 256, bytes_accessed=9 * users * width * 4, transcendentals=0
        ),
        name="within",
    )(owners, keep)


def recur_kernel(packs, rates_hbm, rows_ref, prior_ref, out_ref, rates_ref, sem):
    group = lax.axis_index("hist")
    in_rates = pltpu.make_async_copy(rates_hbm, rates_ref, sem)
    in_rates.start()
    half = packs // 2
    load = lambda part, late: rows_ref[pl.ds(late * half * PARTS + part, half, stride=PARTS), :]
    both = lambda part: [load(part + rank, late) for late in range(2) for rank in range(2)]
    lane = iota((1, 128), 1)
    first = lane < 64

    keys = both(2)
    gap = jnp.concatenate([jnp.broadcast_to(keys[n][:, 0:1], (half, 128)) for n in (1, 3)], axis=0)
    reached = (iota((packs, packs), 0) >= iota((packs, packs), 1)).astype(F32).astype(BF16)
    ended = mm(reached, gap.astype(BF16))
    started = ended - gap
    ended_row = ended.T[0:1, :]
    earlier = iota((half, half), 0) > iota((half, half), 1)
    since = {}
    for late in range(2):
        for source in range(late + 1):
            gone = started[late * half : (late + 1) * half] - ended_row[:, source * half : (source + 1) * half]
            since[late, source] = jnp.where(earlier, gone, 1e30) if late == source else gone

    keys = [jnp.where(lane == 0, 0.0, rows) if n % 2 else rows for n, rows in enumerate(keys)]
    query, key, value = [jnp.concatenate(rows, axis=0) for rows in (both(0), keys, both(4))]
    turned_query, turned_key = pltpu.roll(query, 64, 1), pltpu.roll(key, 64, 1)
    value_high, value_low = split(value)
    value_both = jnp.concatenate([value_high, value_low], axis=1)
    in_rates.wait()
    rate = [rates_ref[2 * group], rates_ref[2 * group + 1]]

    def pieces(x):
        high = x.astype(BF16).astype(F32)
        return high, x - high

    sides = []
    for head in range(2):
        mine = first if head == 0 else jnp.logical_not(first)
        q_high, q_low = pieces(jnp.where(mine, query, turned_query))
        k_high, k_low = pieces(jnp.where(mine, key, turned_key))
        left = jnp.concatenate(
            [jnp.where(first, q_high, q_low), jnp.where(first, q_high, 0.0)], axis=1
        )
        right = jnp.concatenate([k_high, jnp.where(first, k_low, 0.0)], axis=1)
        sides.append((left.astype(BF16), right.astype(BF16)))

    empty = jnp.zeros((64, 64), F32)
    prior = jnp.concatenate(
        [
            jnp.concatenate([prior_ref[2 * group], empty], axis=1),
            jnp.concatenate([empty, prior_ref[2 * group + 1]], axis=1),
        ],
        axis=0,
    )
    prior_high, prior_low = split(prior)
    prior_twice = jnp.concatenate([prior_high, prior_high], axis=0)
    lane_rate = jnp.where(first, rate[0], rate[1])

    for late in range(2):
        mine = slice(late * packs, (late + 1) * packs)
        seen = slice(0, (late + 1) * packs)
        heads = []
        for head in range(2):
            left, right = sides[head]
            fades = []
            for source in range(late + 1):
                fades += [jnp.exp(-rate[head] * since[late, source])] * 2
            fades = jnp.concatenate(fades, axis=1)
            scores = mm(left[mine], right[seen], NT) * jnp.concatenate([fades, fades], axis=0)
            s_high, s_low = split(scores)
            wide = mm(s_high, value_both[seen])
            heads.append(wide[:, :128] + (wide[:, 128:] + mm(s_low, value_high[seen])))
        fade = jnp.exp(-lane_rate * started[late * half : (late + 1) * half])
        f_high, f_low = split(query[mine] * jnp.concatenate([fade, fade], axis=0))
        carried = mm(jnp.concatenate([f_high, f_low], axis=1), prior_twice) + mm(f_high, prior_low)
        result = jnp.where(first, heads[0], heads[1]) + carried
        for rank in range(2):
            out_ref[pl.ds(late * packs + rank, half, stride=2), :] = (
                result[rank * half : (rank + 1) * half]
            )


def recur(rates, rows, prior, packs):
    return pl.pallas_call(
        functools.partial(recur_kernel, packs),
        in_specs=[
            pl.BlockSpec(memory_space=pl.ANY),
            pl.BlockSpec(memory_space=pltpu.VMEM),
            pl.BlockSpec(memory_space=pltpu.VMEM),
        ],
        out_shape=jax.ShapeDtypeStruct((2 * packs, 128), F32),
        scratch_shapes=[pltpu.SMEM(rates.shape, F32), pltpu.SemaphoreType.DMA],
        compiler_params=pltpu.CompilerParams(vmem_limit_bytes=40 * 1024 * 1024),
        name="recur",
    )(rates, rows, prior)


def pick_kernel(users, groups, chosen_ref, rows_ref, within_ref, out_ref):
    chosen = chosen_ref[...].astype(BF16)
    mine = within_ref[...] + jnp.concatenate(
        [
            jnp.concatenate(
                [
                    rows_ref[pl.ds(group * users * 2 + rank, users, stride=2), :]
                    for rank in range(2)
                ],
                axis=0,
            )
            for group in range(groups)
        ],
        axis=1,
    )
    high = mine.astype(BF16)
    middle, low = split(mine - high.astype(F32))
    out_ref[...] = mm(chosen, high) + (mm(chosen, middle) + mm(chosen, low))


def pick(chosen, rows, inside, users, groups):
    return pl.pallas_call(
        functools.partial(pick_kernel, users, groups),
        in_specs=[
            pl.BlockSpec(memory_space=pltpu.VMEM),
            pl.BlockSpec(memory_space=pltpu.VMEM),
            pl.BlockSpec(memory_space=pltpu.VMEM),
        ],
        out_shape=jax.ShapeDtypeStruct((SPP, groups * 128), F32),
        compiler_params=pltpu.CompilerParams(vmem_limit_bytes=16 * 1024 * 1024),
        name="pick",
    )(chosen, rows, inside)


def shards(events, w_qkv, patterns, owners, gaps, rates, prior_state):
    groups = lax.axis_size("hist")
    users = lax.axis_size("sess")
    packs = groups * users
    axes = ("hist", "sess")
    send, keep = encode(
        events[0, 0], w_qkv, patterns[0], owners[0], gaps[0], rates, users, groups
    )
    arrived = lax.all_to_all(
        send.reshape(packs, PARTS, 1, 128), axes, split_axis=0, concat_axis=0, tiled=True
    ).reshape(packs * PARTS, 128)
    inside, chosen = within(owners[0], keep, users)
    arrived, inside, chosen = lax.optimization_barrier((arrived, inside, chosen))
    done = recur(rates, arrived, prior_state[0], packs)
    returned = lax.all_to_all(
        done.reshape(packs, 2, 128), axes, split_axis=0, concat_axis=0, tiled=True
    ).reshape(packs * 2, 128)
    return pick(chosen, returned, inside, users, groups)[None, None]


def solution(mesh):
    placed = (
        P("hist", "sess", None, None),
        P(),
        P("hist", "sess", None),
        P("hist", "sess", None),
        P("hist", "sess", None),
        P(),
        P("sess", None, None, None),
    )
    return jax.shard_map(
        shards, mesh=mesh, in_specs=placed, out_specs=P("hist", "sess", None, None), check_vma=False
    )
```

```python
import functools

import jax
import jax.numpy as jnp
from jax import lax
from jax.experimental import pallas as pl
from jax.experimental.pallas import tpu as pltpu
from jax.sharding import PartitionSpec as P

HEADS = 16
SPP = 32
LONGEST = 48
QUERIES = 64
PARTS = 6
BF16 = jnp.bfloat16
F32 = jnp.float32
NT = (((1,), (1,)), ((), ()))
TN = (((0,), (0,)), ((), ()))


def iota(shape, dim):
    return lax.broadcasted_iota(jnp.int32, shape, dim)


def mm(a, b, dims=(((1,), (0,)), ((), ()))):
    return lax.dot_general(a, b, dims, preferred_element_type=F32)


def split(x):
    high = x.astype(BF16)
    return high, (x - high.astype(F32)).astype(BF16)


def mm3(a, b, dims=(((1,), (0,)), ((), ()))):
    a_high, a_low = split(a)
    b_high, b_low = split(b)
    return mm(a_high, b_high, dims) + (mm(a_low, b_high, dims) + mm(a_high, b_low, dims))


def same_head(columns):
    shape = (columns, columns)
    return (iota(shape, 0) // 64 == iota(shape, 1) // 64).astype(F32).astype(BF16)


def slots_of(owner_row, users):
    owned = owner_row == iota((users, SPP), 0)
    earlier = (iota((SPP, SPP), 0) < iota((SPP, SPP), 1)).astype(BF16)
    before = mm(owned.astype(F32).astype(BF16), earlier)
    return [(owned & (before == float(rank))).astype(F32) for rank in range(2)]


def windows(length):
    result = []
    for start in range(0, length, QUERIES):
        low, high = max(0, start - LONGEST), min(length, start + QUERIES + LONGEST)
        result.append((start, low, high - low))
    return result


def encode_kernel(
    users,
    groups,
    events_hbm,
    w_hbm,
    pattern_hbm,
    owner_hbm,
    gap_hbm,
    rates_hbm,
    send_hbm,
    keep_hbm,
    send_ref,
    keep_ref,
    fade_ref,
    rows_ref,
    w_ref,
    pattern_ref,
    owner_ref,
    gap_ref,
    rates_ref,
    mask_ref,
    query_ref,
    key_ref,
    value_ref,
    weight_ref,
    small_sem,
    events_sem,
    w_sem,
    out_sem,
):
    length, width = events_hbm.shape
    columns = 256
    here = columns // 64
    steps = width // columns
    subs = columns // 128
    chunk = subs * users * PARTS
    small = [
        pltpu.make_async_copy(source, target, small_sem.at[n])
        for n, (source, target) in enumerate(
            [
                (pattern_hbm, pattern_ref),
                (owner_hbm, owner_ref),
                (gap_hbm, gap_ref),
                (rates_hbm, rates_ref),
            ]
        )
    ]
    in_events = pltpu.make_async_copy(events_hbm, rows_ref.at[0:length], events_sem)
    in_w = [
        [
            pltpu.make_async_copy(
                w_hbm.at[:, part * width + step * columns : part * width + (step + 1) * columns],
                w_ref.at[step * 3 + part],
                w_sem.at[step * 3 + part],
            )
            for part in range(3)
        ]
        for step in range(steps)
    ]
    out_keys = pltpu.make_async_copy(
        keep_ref.at[2 * users :], keep_hbm.at[2 * users :], out_sem.at[steps]
    )
    out_queries = pltpu.make_async_copy(
        keep_ref.at[0 : 2 * users], keep_hbm.at[0 : 2 * users], out_sem.at[steps + 1]
    )
    out = [
        pltpu.make_async_copy(
            send_ref.at[step * chunk : (step + 1) * chunk],
            send_hbm.at[step * chunk : (step + 1) * chunk],
            out_sem.at[step],
        )
        for step in range(steps)
    ]
    for copy in small:
        copy.start()
    in_events.start()
    for copy in in_w[0]:
        copy.start()
    for copy in small:
        copy.wait()

    pattern = pattern_ref[...]
    members = (pattern == iota((SPP, length), 0)).astype(F32).astype(BF16)
    slots = slots_of(owner_ref[...], users)
    place = mm(jnp.concatenate(slots, axis=0).astype(BF16), members)
    counts = jnp.sum(place, axis=1, keepdims=True)
    place = place.astype(BF16)
    inverse = jnp.broadcast_to(1.0 / jnp.maximum(counts, 1.0), (2 * users, columns))
    for copies in in_w[1:4]:
        for copy in copies:
            copy.start()
    ids = iota((SPP, 128), 0).astype(F32).astype(BF16)
    id_column = mm(members, ids, TN)
    id_row = pattern.astype(F32)
    offset = 0
    for start, low, size in windows(length):
        block = id_row[:, start : start + QUERIES]
        same = id_column[low : low + size] == jnp.concatenate([block, block], axis=1)
        mask_ref[offset : offset + size, :] = jnp.where(same, 0.0, -jnp.inf)
        offset += size
    gap_row = gap_ref[...].astype(F32)
    gaps = [jnp.sum(slot * gap_row, axis=1, keepdims=True) for slot in slots]
    lane = iota((1, 128), 1)
    first = lane < 64
    for group in range(groups):
        at = slice(group * 128, (group + 1) * 128)
        rate = jnp.where(first, rates_ref[2 * group], rates_ref[2 * group + 1])
        fade_ref[0:users, at] = jnp.exp(-rate * gaps[0])
        fade_ref[users:, at] = jnp.exp(-rate * (gaps[0] + gaps[1]))
        keep_ref[6 * users :, at] = jnp.exp(-rate * gaps[1])

    head_of = iota((1, columns), 1) // 64
    only = [jnp.where(head_of == head, 0.125, 0.0).astype(BF16) for head in range(here)]
    spread = same_head(columns)

    def put(group, part, rows):
        for rank in range(2):
            send_ref[pl.ds(group * users * PARTS + part * 2 + rank, users, stride=PARTS), :] = rows[
                rank
            ]

    def project(step):
        for part, target in enumerate((query_ref, key_ref, value_ref)):
            for at in range(0, length, 256):
                rows = rows_ref[at : at + 256, :]
                target[step, at : at + 256, :] = mm(rows, w_ref[step * 3 + part]).astype(BF16)

    def average(step):
        means = []
        for part in (1, 2):
            both = mm(rows_ref[length:, :], w_ref[step * 3 + part])
            mean = (both[: 2 * users] + both[2 * users :]) * inverse
            keep_ref[
                2 * part * users : 2 * (part + 1) * users, step * columns : (step + 1) * columns
            ] = mean
            means.append(mean)
        for sub in range(subs):
            group = step * subs + sub
            key, later_key, value, later_value = [
                mean[rank * users : (rank + 1) * users, sub * 128 : (sub + 1) * 128]
                for mean in means
                for rank in range(2)
            ]
            key = key * keep_ref[6 * users :, group * 128 : (group + 1) * 128]
            x, y = key[:, 0:1], later_key[:, 0:1]
            size = jnp.maximum(jnp.abs(x), jnp.abs(y))
            some = size > 0.0
            size = jnp.where(some, size, 1.0)
            x, y = jnp.where(some, x / size, 1.0), y / size
            norm = jnp.sqrt(x * x + y * y)
            cosine = jnp.where(first, x / norm, 1.0)
            sine = jnp.where(first, y / norm, 0.0)
            turned = cosine * later_key - sine * key
            total = gaps[0] + gaps[1]
            put(group, 1, (cosine * key + sine * later_key, jnp.where(lane == 0, total, turned)))
            put(
                group,
                2,
                (cosine * value + sine * later_value, cosine * later_value - sine * value),
            )

    def attend(step):
        offset = 0
        reached = 0
        for start, low, size in windows(length):
            block = query_ref[step, start : start + QUERIES, :]
            stacked = jnp.concatenate([block * keep for keep in only], axis=0)
            scores = mm(key_ref[step, low : low + size, :], stacked, NT)
            mask = mask_ref[offset : offset + size, :]
            offset += size
            probs = []
            for half in range(columns // 128):
                part = scores[:, half * 128 : (half + 1) * 128] + mask
                expd = jnp.exp(part - jnp.max(part, axis=0, keepdims=True))
                probs.append(expd * (1.0 / jnp.sum(expd, axis=0, keepdims=True)))
            probs = jnp.concatenate(probs, axis=1)
            known = reached - low
            if known:
                weight_ref[step, low:reached, :] += probs[:known]
            weight_ref[step, reached : low + size, :] = probs[known:]
            reached = low + size

    def finish(step):
        mean = None
        for at in range(0, length, 128):
            weight = mm(weight_ref[step, at : at + 128, :].astype(BF16), spread)
            high, low = split(weight * value_ref[step, at : at + 128, :].astype(F32))
            some = mm(place[:, at : at + 128], high) + mm(place[:, at : at + 128], low)
            mean = some if mean is None else mean + some
        mean = mean * inverse
        keep_ref[0 : 2 * users, step * columns : (step + 1) * columns] = mean
        for sub in range(subs):
            group = step * subs + sub
            faded = mean[:, sub * 128 : (sub + 1) * 128] * fade_ref[
                :, group * 128 : (group + 1) * 128
            ]
            put(group, 0, (faded[:users], faded[users:]))

    in_events.wait()
    for copy in in_w[0]:
        copy.wait()
    high, low = split(mm(place, rows_ref[0:length, :]))
    rows_ref[length : length + 2 * users, :] = high
    rows_ref[length + 2 * users :, :] = low
    project(0)
    for copies in in_w[1:2]:
        for copy in copies:
            copy.wait()
    project(1)
    for copies in in_w[2:4]:
        for copy in copies:
            copy.wait()
    attend(0)
    average(0)
    attend(1)
    average(1)
    project(2)
    attend(2)
    average(2)
    project(3)
    attend(3)
    average(3)
    finish(0)
    finish(1)
    out_keys.start()
    out[0].start()
    out[1].start()
    finish(2)
    out[2].start()
    finish(3)
    out[3].start()
    out_queries.start()
    for copy in [out_keys, out_queries] + out:
        copy.wait()


def encode(events, w_qkv, patterns, owners, gaps, rates, users, groups):
    length, width = events.shape
    columns = 256
    steps = width // columns
    window_rows = sum(size for _, _, size in windows(length))
    send = jax.ShapeDtypeStruct((groups * users * PARTS, 128), F32)
    keep = jax.ShapeDtypeStruct((7 * users, width), F32)
    return pl.pallas_call(
        functools.partial(encode_kernel, users, groups),
        in_specs=[pl.BlockSpec(memory_space=pl.ANY)] * 6,
        out_specs=[pl.BlockSpec(memory_space=pl.ANY)] * 2,
        out_shape=[send, keep],
        scratch_shapes=[
            pltpu.VMEM(send.shape, F32),
            pltpu.VMEM(keep.shape, F32),
            pltpu.VMEM((2 * users, width), F32),
            pltpu.VMEM((length + 4 * users, width), BF16),
            pltpu.VMEM((3 * steps, width, columns), BF16),
            pltpu.VMEM((1, length), jnp.int32),
            pltpu.VMEM((1, SPP), jnp.int32),
            pltpu.VMEM((1, SPP), jnp.int32),
            pltpu.SMEM(rates.shape, F32),
            pltpu.VMEM((window_rows, 128), F32),
            pltpu.VMEM((steps, length, columns), BF16),
            pltpu.VMEM((steps, length, columns), BF16),
            pltpu.VMEM((steps, length, columns), BF16),
            pltpu.VMEM((steps, length, columns), F32),
            pltpu.SemaphoreType.DMA((4,)),
            pltpu.SemaphoreType.DMA,
            pltpu.SemaphoreType.DMA((3 * steps,)),
            pltpu.SemaphoreType.DMA((steps + 2,)),
        ],
        compiler_params=pltpu.CompilerParams(vmem_limit_bytes=60 * 1024 * 1024),
        name="encode",
    )(events, w_qkv, patterns, owners, gaps, rates)


def within_kernel(users, owner_ref, keep_ref, out_ref, chosen_ref):
    query, later_query, key, later_key, value, later_value, fade = [
        keep_ref[n * users : (n + 1) * users, :] for n in range(7)
    ]
    products = jnp.concatenate([query * key, later_query * key, later_query * later_key], axis=0)
    chosen_ref[...] = jnp.concatenate(slots_of(owner_ref[...], users), axis=0).T
    columns = 256
    spread = same_head(columns)
    for at in range(0, products.shape[1], columns):
        here = slice(at, at + columns)
        part = products[:, here]
        high = part.astype(BF16)
        middle, low = split(part - high.astype(F32))
        dots = mm(high, spread) + (mm(middle, spread) + mm(low, spread))
        out_ref[:users, here] = dots[:users] * value[:, here]
        out_ref[users:, here] = (
            fade[:, here] * dots[users : 2 * users] * value[:, here]
            + dots[2 * users :] * later_value[:, here]
        )


def within(owners, keep, users):
    width = keep.shape[1]
    return pl.pallas_call(
        functools.partial(within_kernel, users),
        out_shape=[
            jax.ShapeDtypeStruct((2 * users, width), F32),
            jax.ShapeDtypeStruct((SPP, 2 * users), F32),
        ],
        compiler_params=pltpu.CompilerParams(vmem_limit_bytes=16 * 1024 * 1024),
        cost_estimate=pl.CostEstimate(
            flops=2 * 9 * users * width * 256, bytes_accessed=9 * users * width * 4, transcendentals=0
        ),
        name="within",
    )(owners, keep)


def recur_kernel(packs, rates_hbm, rows_ref, prior_ref, out_ref, rates_ref, sem):
    group = lax.axis_index("hist")
    in_rates = pltpu.make_async_copy(rates_hbm, rates_ref, sem)
    in_rates.start()
    half = packs // 2
    load = lambda part, late: rows_ref[pl.ds(late * half * PARTS + part, half, stride=PARTS), :]
    both = lambda part: [load(part + rank, late) for late in range(2) for rank in range(2)]
    lane = iota((1, 128), 1)
    first = lane < 64

    keys = both(2)
    gap = jnp.concatenate([jnp.broadcast_to(keys[n][:, 0:1], (half, 128)) for n in (1, 3)], axis=0)
    reached = (iota((packs, packs), 0) >= iota((packs, packs), 1)).astype(F32).astype(BF16)
    ended = mm(reached, gap.astype(BF16))
    started = ended - gap
    ended_row = ended.T[0:1, :]
    earlier = iota((half, half), 0) > iota((half, half), 1)
    since = {}
    for late in range(2):
        for source in range(late + 1):
            gone = started[late * half : (late + 1) * half] - ended_row[:, source * half : (source + 1) * half]
            since[late, source] = jnp.where(earlier, gone, 1e30) if late == source else gone

    keys = [jnp.where(lane == 0, 0.0, rows) if n % 2 else rows for n, rows in enumerate(keys)]
    query, key, value = [jnp.concatenate(rows, axis=0) for rows in (both(0), keys, both(4))]
    turned_query, turned_key = pltpu.roll(query, 64, 1), pltpu.roll(key, 64, 1)
    value_high, value_low = split(value)
    value_both = jnp.concatenate([value_high, value_low], axis=1)
    in_rates.wait()
    rate = [rates_ref[2 * group], rates_ref[2 * group + 1]]

    def pieces(x):
        high = x.astype(BF16).astype(F32)
        return high, x - high

    sides = []
    for head in range(2):
        mine = first if head == 0 else jnp.logical_not(first)
        q_high, q_low = pieces(jnp.where(mine, query, turned_query))
        k_high, k_low = pieces(jnp.where(mine, key, turned_key))
        left = jnp.concatenate(
            [jnp.where(first, q_high, q_low), jnp.where(first, q_high, 0.0)], axis=1
        )
        right = jnp.concatenate([k_high, jnp.where(first, k_low, 0.0)], axis=1)
        sides.append((left.astype(BF16), right.astype(BF16)))

    empty = jnp.zeros((64, 64), F32)
    prior = jnp.concatenate(
        [
            jnp.concatenate([prior_ref[2 * group], empty], axis=1),
            jnp.concatenate([empty, prior_ref[2 * group + 1]], axis=1),
        ],
        axis=0,
    )
    prior_high, prior_low = split(prior)
    prior_twice = jnp.concatenate([prior_high, prior_high], axis=0)
    lane_rate = jnp.where(first, rate[0], rate[1])

    total = [None, None]
    for source in range(2):
        seen = slice(source * packs, (source + 1) * packs)
        later = range(source, 2)
        scores = []
        for head in range(2):
            left, right = sides[head]
            fades = []
            for late in later:
                fade = jnp.exp(-rate[head] * since[late, source])
                fade = jnp.concatenate([fade, fade], axis=1)
                fades += [fade, fade]
            scores.append(
                mm(left[source * packs :], right[seen], NT) * jnp.concatenate(fades, axis=0)
            )
        s_high, s_low = split(jnp.concatenate(scores, axis=1))
        stacked = jnp.concatenate(
            [jnp.where(first, value[seen], 0.0), jnp.where(first, 0.0, value[seen])], axis=0
        )
        v_high, v_low = split(stacked)
        wide = mm(s_high, jnp.concatenate([v_high, v_low], axis=1))
        part = wide[:, :128] + (wide[:, 128:] + mm(s_low, v_high))
        for late in later:
            some = part[(late - source) * packs : (late - source + 1) * packs]
            total[late] = some if total[late] is None else total[late] + some
    for late in range(2):
        mine = slice(late * packs, (late + 1) * packs)
        fade = jnp.exp(-lane_rate * started[late * half : (late + 1) * half])
        f_high, f_low = split(query[mine] * jnp.concatenate([fade, fade], axis=0))
        carried = mm(jnp.concatenate([f_high, f_low], axis=1), prior_twice) + mm(f_high, prior_low)
        result = total[late] + carried
        for rank in range(2):
            out_ref[pl.ds(late * packs + rank, half, stride=2), :] = (
                result[rank * half : (rank + 1) * half]
            )


def recur(rates, rows, prior, packs):
    return pl.pallas_call(
        functools.partial(recur_kernel, packs),
        in_specs=[
            pl.BlockSpec(memory_space=pl.ANY),
            pl.BlockSpec(memory_space=pltpu.VMEM),
            pl.BlockSpec(memory_space=pltpu.VMEM),
        ],
        out_shape=jax.ShapeDtypeStruct((2 * packs, 128), F32),
        scratch_shapes=[pltpu.SMEM(rates.shape, F32), pltpu.SemaphoreType.DMA],
        compiler_params=pltpu.CompilerParams(vmem_limit_bytes=40 * 1024 * 1024),
        name="recur",
    )(rates, rows, prior)


def pick_kernel(users, groups, chosen_ref, rows_ref, within_ref, out_ref):
    chosen = chosen_ref[...].astype(BF16)
    mine = within_ref[...] + jnp.concatenate(
        [
            jnp.concatenate(
                [
                    rows_ref[pl.ds(group * users * 2 + rank, users, stride=2), :]
                    for rank in range(2)
                ],
                axis=0,
            )
            for group in range(groups)
        ],
        axis=1,
    )
    high = mine.astype(BF16)
    middle, low = split(mine - high.astype(F32))
    out_ref[...] = mm(chosen, high) + (mm(chosen, middle) + mm(chosen, low))


def pick(chosen, rows, inside, users, groups):
    return pl.pallas_call(
        functools.partial(pick_kernel, users, groups),
        in_specs=[
            pl.BlockSpec(memory_space=pltpu.VMEM),
            pl.BlockSpec(memory_space=pltpu.VMEM),
            pl.BlockSpec(memory_space=pltpu.VMEM),
        ],
        out_shape=jax.ShapeDtypeStruct((SPP, groups * 128), F32),
        compiler_params=pltpu.CompilerParams(vmem_limit_bytes=16 * 1024 * 1024),
        name="pick",
    )(chosen, rows, inside)


def shards(events, w_qkv, patterns, owners, gaps, rates, prior_state):
    groups = lax.axis_size("hist")
    users = lax.axis_size("sess")
    packs = groups * users
    axes = ("hist", "sess")
    send, keep = encode(
        events[0, 0], w_qkv, patterns[0], owners[0], gaps[0], rates, users, groups
    )
    arrived = lax.all_to_all(
        send.reshape(packs, PARTS, 1, 128), axes, split_axis=0, concat_axis=0, tiled=True
    ).reshape(packs * PARTS, 128)
    inside, chosen = within(owners[0], keep, users)
    arrived, inside, chosen = lax.optimization_barrier((arrived, inside, chosen))
    done = recur(rates, arrived, prior_state[0], packs)
    returned = lax.all_to_all(
        done.reshape(packs, 2, 128), axes, split_axis=0, concat_axis=0, tiled=True
    ).reshape(packs * 2, 128)
    return pick(chosen, returned, inside, users, groups)[None, None]


def solution(mesh):
    placed = (
        P("hist", "sess", None, None),
        P(),
        P("hist", "sess", None),
        P("hist", "sess", None),
        P("hist", "sess", None),
        P(),
        P("sess", None, None, None),
    )
    return jax.shard_map(
        shards, mesh=mesh, in_specs=placed, out_specs=P("hist", "sess", None, None), check_vma=False
    )
```
